32 devices in a mesh: groups: 2 (over y), dp: 4 (over z), tensor: 2 (over x), seq: 2 (over core).
Axes of the slice: x: 2, y: 2, z: 4, core: 2. Of those that a mesh axis runs over, the one named last changes fastest.
Arguments:
- saved_layer_input: bfloat16 [2048, 5120], P(('groups', 'dp', 'seq'), 'tensor'), parts along dimension 0, may hold values from -6 to 6
- output_gradient: bfloat16 [2048, 2560], P(('groups', 'dp', 'seq'), 'tensor'), parts along dimension 0, may hold values from -6 to 6
- adapter_of_row: int32 [2048], P(('groups', 'dp')), parts along dimension 0, may hold values from 0 to 3, as said below
- adapter_owner_slot: int32 [8], P('groups'), parts along dimension 0, may hold values from 0 to 7, as said below
- frozen_query_weight: bfloat16 [5120, 2560], P(('dp', 'seq'), 'tensor'), may hold values from -0.078125 to 0.078125
- adapter_down_factors: bfloat16 [10240, 4, 16], P(('groups', 'tensor')), parts along dimension 0, may hold values from -0.078125 to 0.078125
- adapter_up_factors: bfloat16 [8, 16, 2560], P('groups', None, 'tensor'), parts along dimension 0, may hold values from -0.125 to 0.125
Outputs:
- input_gradient: bfloat16 [2048, 5120], P(('groups', 'dp', 'seq'), 'tensor'), parts along dimension 0
- down_grad: float32 [10240, 8, 16], P(('groups', 'tensor', 'seq'), 'dp'), parts along dimension 0
- up_grad: float32 [16, 16, 2560], P(('groups', 'dp'), None, ('tensor', 'seq')), parts along dimension 0
The draws below stay inside these ranges and needn't reach their ends.
There are 2 independent parts, one for each index of `groups`. The reference program is written for one: setup_inputs(seed, part) draws one part's arguments, and reference() takes and returns one part's arrays. A program takes and returns all parts, laid end to end along the dimension named above; an argument that names none is the same for every part. Nothing has to cross between parts.
Inputs may be any that keep to these rules, and one draw needn't show every extreme that they name: `adapter_of_row`: within each aligned block of 128 rows the ids do not fall; every adapter is named by at least one row. `adapter_owner_slot`: distinct slots; the owner of slot s is index s // 2 of dp; some owner has all 2 of its slots taken.
All inputs are finite; a program needn't handle non-finite values.
Results may differ from the reference program's by a relative error of at most 0.017.
Values may be sent and summed in bfloat16 or wider, within the bound.
No kernel may reach another device: no remote copies, remote signals or barrier semaphores. Data moves between devices by JAX's collectives and lax.ppermute only.
A program may use at most 64 MiB of HBM per device.

```python
import jax
import jax.numpy as jnp
from jax import lax

MODEL_WIDTH = 5120
QUERY_COLUMNS = 2560
ADAPTER_RANK = 16
OWN_MAX = 2
TOK_DEV = 128
TOKEN_ROWS = 1024
ADAPTER_COUNT = 4
SLOTS = 8
N_TENSOR = 2


def draw_adapter_of_row(key, part):
    key = jax.random.fold_in(key, 11)
    key_uniform, key_hot, key_dice = jax.random.split(key, 3)
    chip_rows = 2 * TOK_DEV
    chip_total = TOKEN_ROWS // chip_rows
    uniform_ids = jax.random.randint(key_uniform, (TOKEN_ROWS,), 0, ADAPTER_COUNT)
    hot_adapter = jax.random.randint(key_hot, (), 0, ADAPTER_COUNT)
    positions = jnp.arange(TOKEN_ROWS, dtype=jnp.int32)
    chip_of_row = positions // chip_rows
    chance = 100 + 300 * chip_of_row // max(chip_total - 1, 1)
    dice_roll = jax.random.randint(key_dice, (TOKEN_ROWS,), 0, 1000)
    chosen = jnp.where(dice_roll < chance, hot_adapter, uniform_ids)
    chosen = jnp.where(positions < ADAPTER_COUNT, positions, chosen)
    blocks = chosen.reshape(TOKEN_ROWS // TOK_DEV, TOK_DEV)
    return jnp.sort(blocks, axis=1).reshape(TOKEN_ROWS).astype(jnp.int32)


def draw_adapter_owner_slot(key, part):
    key = jax.random.fold_in(key, 23)
    key_rest, key_rotation, key_order = jax.random.split(key, 3)
    remainder = jax.random.permutation(key_rest, SLOTS - OWN_MAX) + OWN_MAX
    chosen = jnp.concatenate([jnp.arange(OWN_MAX, dtype=jnp.int32), remainder[:ADAPTER_COUNT - OWN_MAX].astype(jnp.int32)])
    rotation = jax.random.randint(key_rotation, (), 0, ADAPTER_COUNT) * OWN_MAX
    chosen = (chosen + rotation) % SLOTS
    return jax.random.permutation(key_order, chosen).astype(jnp.int32)


def levels(own_key, dims, cuts, low, high):
    def one(dim, shards_of):
        heights = jax.random.uniform(jax.random.fold_in(jax.random.fold_in(own_key, 6), dim), (shards_of,), jnp.float32, low / len(cuts), high / len(cuts))
        return jnp.repeat(jnp.exp(heights), dims[dim] // shards_of).reshape((-1,) + (1,) * (len(dims) - dim - 1))

    loudness = one(*cuts[0])
    for cut in cuts[1:]:
        loudness = loudness * one(*cut)
    return loudness


def noise(stream_key, extent, scale, limit, cuts=(), held_as=jnp.bfloat16):
    array = scale * jax.random.normal(stream_key, extent, jnp.float32)
    if cuts:
        array = array * levels(stream_key, extent, cuts, -0.22, 0.18)
    return jnp.clip(array, -limit, limit).astype(held_as)


def setup_inputs(seed: int = 0, part: int = 0) -> dict:
    key_list = jax.random.split(jax.random.key(seed), 8)
    part_keys = jax.random.split(jax.random.fold_in(key_list[7], part), 8)
    return {
        "saved_layer_input": noise(part_keys[0], (TOKEN_ROWS, MODEL_WIDTH), 1.0, 6.0, ((0, 8), (1, 2))),
        "output_gradient": noise(part_keys[1], (TOKEN_ROWS, QUERY_COLUMNS), 1.0, 6.0, ((0, 8), (1, 2))),
        "adapter_of_row": draw_adapter_of_row(jax.random.fold_in(jax.random.fold_in(key_list[7], part), 71), part),
        "adapter_owner_slot": draw_adapter_owner_slot(jax.random.fold_in(jax.random.fold_in(key_list[7], part), 71), part),
        "frozen_query_weight": noise(key_list[4], (MODEL_WIDTH, QUERY_COLUMNS), MODEL_WIDTH ** -0.5, 0.078125, ((0, 8), (1, 2))),
        "adapter_down_factors": noise(part_keys[5], (MODEL_WIDTH, ADAPTER_COUNT, ADAPTER_RANK), MODEL_WIDTH ** -0.5, 0.078125, ((0, 2),)),
        "adapter_up_factors": noise(part_keys[6], (ADAPTER_COUNT, ADAPTER_RANK, QUERY_COLUMNS), QUERY_COLUMNS ** -0.5, 0.125, ((2, 2),)),
    }


adapter_scale = 2.0


def contract_final_axis(left_side, right_side):
    return lax.dot_general(left_side, right_side, (((1,), (1,)), ((), ())), preferred_element_type=jnp.float32)


def contract_rows(left_side, right_side):
    return lax.dot_general(left_side, right_side, (((0,), (0,)), ((), ())), preferred_element_type=jnp.float32)


def reference(saved_layer_input, output_gradient, adapter_of_row, adapter_owner_slot, frozen_query_weight, adapter_down_factors, adapter_up_factors):
    labels = jnp.arange(ADAPTER_COUNT, dtype=jnp.int32)
    matches = (adapter_of_row[:, None] == labels[None, :]).astype(jnp.int32)
    counts = jnp.sum(matches, axis=0)
    per_adapter = jnp.float32(TOKEN_ROWS) / (jnp.float32(ADAPTER_COUNT) * counts.astype(jnp.float32))
    match_float = matches.astype(jnp.float32)
    row_balance_weight = jnp.sum(match_float * per_adapter[None, :], axis=1)
    column_block = QUERY_COLUMNS // N_TENSOR
    frozen_sum = jnp.zeros((TOKEN_ROWS, MODEL_WIDTH), jnp.float32)
    for block_index in range(N_TENSOR):
        lower = block_index * column_block
        upper = lower + column_block
        term = contract_final_axis(output_gradient[:, lower:upper], frozen_query_weight[:, lower:upper])
        rounded = lax.optimization_barrier(term.astype(jnp.bfloat16))
        frozen_sum = frozen_sum + rounded.astype(jnp.float32)
    into_everyone = jnp.dot(saved_layer_input, adapter_down_factors.reshape(MODEL_WIDTH, ADAPTER_COUNT * ADAPTER_RANK), preferred_element_type=jnp.float32).reshape(TOKEN_ROWS, ADAPTER_COUNT, ADAPTER_RANK)
    output_everyone = contract_final_axis(output_gradient, adapter_up_factors.reshape(ADAPTER_COUNT * ADAPTER_RANK, QUERY_COLUMNS)).reshape(TOKEN_ROWS, ADAPTER_COUNT, ADAPTER_RANK)
    in_sum = jnp.sum(into_everyone * match_float[:, :, None], axis=1)
    output_sum_total = jnp.sum(output_everyone * match_float[:, :, None], axis=1)
    reduced_input = in_sum.astype(jnp.bfloat16)
    reduced_output = (adapter_scale * row_balance_weight[:, None] * output_sum_total).astype(jnp.bfloat16)
    raised_rows = (adapter_scale * row_balance_weight[:, None] * reduced_input.astype(jnp.float32)).astype(jnp.bfloat16)
    distribute_rows = (matches.astype(jnp.bfloat16)[:, :, None] * reduced_output[:, None, :]).reshape(TOKEN_ROWS, ADAPTER_COUNT * ADAPTER_RANK)
    adapter_term = contract_final_axis(distribute_rows, adapter_down_factors.reshape(MODEL_WIDTH, ADAPTER_COUNT * ADAPTER_RANK))
    input_gradient = (row_balance_weight[:, None] * frozen_sum + adapter_term).astype(jnp.bfloat16)
    slot_of_row = jnp.sum(matches * adapter_owner_slot[None, :], axis=1)
    slot_match = (slot_of_row[:, None] == jnp.arange(SLOTS, dtype=jnp.int32)[None, :]).astype(jnp.bfloat16)
    spread_out = (slot_match[:, :, None] * reduced_output[:, None, :]).reshape(TOKEN_ROWS, SLOTS * ADAPTER_RANK)
    spread_in = (slot_match[:, :, None] * raised_rows[:, None, :]).reshape(TOKEN_ROWS, SLOTS * ADAPTER_RANK)
    chip_rows = 2 * TOK_DEV

    def accumulate(totals, chip_index):
        row_start = chip_index * chip_rows
        rows_in = lax.dynamic_slice_in_dim(saved_layer_input, row_start, chip_rows, 0)
        rows_grad = lax.dynamic_slice_in_dim(output_gradient, row_start, chip_rows, 0)
        rows_out = lax.dynamic_slice_in_dim(spread_out, row_start, chip_rows, 0)
        rows_lift = lax.dynamic_slice_in_dim(spread_in, row_start, chip_rows, 0)
        down_term = contract_rows(rows_in, rows_out).astype(jnp.bfloat16)
        up_term = contract_rows(rows_lift, rows_grad).astype(jnp.bfloat16)
        down_term, up_term = lax.optimization_barrier((down_term, up_term))
        return (totals[0] + down_term.astype(jnp.float32), totals[1] + up_term.astype(jnp.float32)), None

    start_totals = (jnp.zeros((MODEL_WIDTH, SLOTS * ADAPTER_RANK), jnp.float32), jnp.zeros((SLOTS * ADAPTER_RANK, QUERY_COLUMNS), jnp.float32))
    final_totals, _ = lax.scan(accumulate, start_totals, jnp.arange(TOKEN_ROWS // chip_rows, dtype=jnp.int32))
    down_grad = final_totals[0].reshape(MODEL_WIDTH, SLOTS, ADAPTER_RANK)
    up_grad = final_totals[1].reshape(SLOTS, ADAPTER_RANK, QUERY_COLUMNS)
    return (input_gradient, down_grad, up_grad)
```

```python
import jax
import jax.numpy as jnp
from jax import lax
from jax.sharding import PartitionSpec as P

OWN_MAX = 2
ADAPTER_SCALE = 2.0
F32 = jnp.float32
BF16 = jnp.bfloat16


def dot_last(left, right):
    return lax.dot_general(left, right, (((1,), (1,)), ((), ())), preferred_element_type=F32)


def dot_plain(left, right):
    return lax.dot_general(left, right, (((1,), (0,)), ((), ())), preferred_element_type=F32)


def shift(value, axis, step):
    size = lax.axis_size(axis)
    return lax.ppermute(value, axis, [(i, (i + step) % size) for i in range(size)])


def pick(value, index):
    return lax.dynamic_index_in_dim(value, index, 0, keepdims=False)


def local(x, g, ids, owner_slot, w, down, up):
    rows = x.shape[0]
    adapters = owner_slot.shape[0]
    rank = up.shape[1]
    n, tensors, cores = lax.axis_size("dp"), lax.axis_size("tensor"), lax.axis_size("seq")
    z, t, c = lax.axis_index("dp"), lax.axis_index("tensor"), lax.axis_index("seq")
    slots = n * OWN_MAX
    labels = jnp.arange(adapters, dtype=jnp.int32)

    blocks = [g] + [shift(g, "dp", s) for s in range(1, n)]
    w_other = lax.ppermute(w, "seq", [(0, 1), (1, 0)])
    w_chip = jnp.concatenate(
        [jnp.where(c == 0, w, w_other), jnp.where(c == 0, w_other, w)], axis=0
    )
    width = w_chip.shape[0]

    down_t = down.transpose(1, 2, 0).reshape(adapters * rank, -1)
    up_t = up.reshape(adapters * rank, -1)
    own_ids = lax.dynamic_slice_in_dim(ids, c * rows, rows, 0)
    own_match = (own_ids[None, :] == labels[:, None]).astype(F32)
    low_in = dot_last(down_t, x).reshape(adapters, rank, rows)
    low_out = dot_last(up_t, g).reshape(adapters, rank, rows)
    low = jnp.concatenate(
        [
            jnp.sum(low_in * own_match[:, None, :], axis=0),
            jnp.sum(low_out * own_match[:, None, :], axis=0),
        ],
        axis=0,
    )
    low_sum = low
    for s in range(1, tensors):
        low_sum = low_sum + shift(low, "tensor", s)
    low_bf = low_sum.astype(BF16)
    low_in, low_out = low_bf[:rank], low_bf[rank:]

    id_rows = ids.reshape(cores, rows).astype(BF16)
    card = jnp.concatenate(
        [low_in, id_rows, jnp.zeros((16 - cores, rows), BF16)], axis=0
    )
    cards = jnp.stack([card] + [shift(card, "dp", s) for s in range(1, n)])
    all_ids = cards[:, rank : rank + cores].astype(jnp.int32)
    counts = jnp.sum(
        (all_ids.reshape(1, -1) == labels[:, None]).astype(F32), axis=1
    )
    weight = F32(n * cores * rows) / (F32(adapters) * counts)

    own_slot = jnp.sum((own_match * owner_slot.astype(F32)[:, None]), axis=0).astype(jnp.int32)
    slot_labels = jnp.arange(slots, dtype=jnp.int32)
    spread = (
        (own_slot[None, :] == slot_labels[:, None]).astype(BF16)[:, None, :] * low_out[None]
    ).reshape(slots * rank, rows)
    down_part = dot_plain(spread, x).astype(BF16)
    half = down_part.shape[1] // cores
    away = lax.dynamic_slice_in_dim(down_part, (1 - c) * half, half, 1)
    mine = lax.dynamic_slice_in_dim(down_part, c * half, half, 1)
    got = lax.ppermute(away, "seq", [(0, 1), (1, 0)])
    chip_part = (mine.astype(F32) + got.astype(F32)).astype(BF16)
    chip_part = chip_part.reshape(n, OWN_MAX * rank, half)
    down_sum = pick(chip_part, z).astype(F32)
    for s in range(1, n):
        down_sum = down_sum + shift(pick(chip_part, (z + s) % n), "dp", s).astype(F32)
    my_slots = z * OWN_MAX + jnp.arange(OWN_MAX, dtype=jnp.int32)
    slot_weight = ADAPTER_SCALE * jnp.sum(
        jnp.where(owner_slot[None, :] == my_slots[:, None], weight[None, :], 0.0), axis=1
    )
    down_grad = down_sum.reshape(OWN_MAX, rank, half) * slot_weight[:, None, None]
    down_grad = down_grad.transpose(2, 0, 1)

    chunk = width // tensors
    back = []
    for s in range(n):
        part = dot_last(blocks[s], w_chip).astype(BF16)
        part = part.reshape(rows, tensors, chunk).transpose(1, 0, 2)
        total = pick(part, t).astype(F32)
        for k in range(1, tensors):
            total = total + shift(pick(part, (t + k) % tensors), "tensor", k).astype(F32)
        total = total.astype(BF16)
        back.append(shift(total, "dp", -s) if s else total)
    span = n // tensors
    groups = []
    for r in range(span):
        stack = jnp.stack([back[r + k * span] for k in range(tensors)])
        first = ((z + r) % n) // span
        order = lambda p: (p - first) % tensors
        pieces = [pick(stack, order(t))]
        for k in range(1, tensors):
            pieces.append(shift(pick(stack, order((t + k) % tensors)), "tensor", k))
        pieces = jnp.stack(pieces)
        groups.append(jnp.stack([pick(pieces, (t - p) % tensors) for p in range(tensors)]))
    groups = jnp.stack(groups)
    base = jnp.stack([pick(groups, (q - z) % span) for q in range(span)])
    base = base.transpose(2, 0, 1, 3).reshape(rows, span * width)

    own_weight = jnp.sum(own_match * weight[:, None], axis=0)
    scattered = (own_match.astype(BF16)[:, None, :] * low_out[None]).reshape(adapters * rank, rows)
    adapter_term = lax.dot_general(
        scattered, down_t, (((0,), (0,)), ((), ())), preferred_element_type=F32
    )
    input_gradient = (
        own_weight[:, None] * (base.astype(F32) + ADAPTER_SCALE * adapter_term)
    ).astype(BF16)

    slot_of = jnp.sum(
        jnp.where(
            lax.dynamic_index_in_dim(all_ids, c, 1, keepdims=False)[:, None, :] == labels[None, :, None],
            owner_slot[None, :, None],
            0,
        ),
        axis=1,
    )
    up_part = jnp.zeros((OWN_MAX * rank, g.shape[1]), F32)
    for s in range(n):
        lift = (
            (slot_of[s][None, :] == my_slots[:, None]).astype(BF16)[:, None, :]
            * cards[s, :rank][None]
        ).reshape(OWN_MAX * rank, rows)
        up_part = up_part + dot_plain(lift, blocks[s])
    up_half = up_part.shape[1] // cores
    up_mine = lax.dynamic_slice_in_dim(up_part, c * up_half, up_half, 1)
    up_away = lax.dynamic_slice_in_dim(up_part, (1 - c) * up_half, up_half, 1)
    up_sum = up_mine + lax.ppermute(up_away, "seq", [(0, 1), (1, 0)])
    up_grad = up_sum.reshape(OWN_MAX, rank, up_half) * slot_weight[:, None, None]
    return input_gradient, down_grad, up_grad


def solution(mesh):
    in_specs = (
        P(("groups", "dp", "seq"), "tensor"),
        P(("groups", "dp", "seq"), "tensor"),
        P(("groups", "dp")),
        P("groups"),
        P(("dp", "seq"), "tensor"),
        P(("groups", "tensor"), None, None),
        P("groups", None, "tensor"),
    )
    out_specs = (
        P(("groups", "dp", "seq"), "tensor"),
        P(("groups", "tensor", "seq"), "dp", None),
        P(("groups", "dp"), None, ("tensor", "seq")),
    )
    return jax.shard_map(local, mesh=mesh, in_specs=in_specs, out_specs=out_specs, check_vma=False)
```

```python
import jax
import jax.numpy as jnp
from jax import lax
from jax.experimental import pallas as pl
from jax.experimental.pallas import tpu as pltpu
from jax.sharding import PartitionSpec as P

OWN_MAX = 2
ADAPTER_SCALE = 2.0
F32 = jnp.float32
BF16 = jnp.bfloat16
VMEM = pl.BlockSpec(memory_space=pltpu.VMEM)
SMEM = pl.BlockSpec(memory_space=pltpu.SMEM)
ANY = pl.BlockSpec(memory_space=pl.ANY)


def dot_last(left, right):
    return lax.dot_general(left, right, (((1,), (1,)), ((), ())), preferred_element_type=F32)


def dot_plain(left, right):
    return lax.dot_general(left, right, (((1,), (0,)), ((), ())), preferred_element_type=F32)


def dot_first(left, right):
    return lax.dot_general(left, right, (((0,), (0,)), ((), ())), preferred_element_type=F32)


def call(body, out_shape, args, specs, out_specs=None, scratch=(), aliases=None):
    in_specs = [specs.get(i, VMEM) for i in range(len(args))]
    if out_specs is None:
        out_specs = jax.tree.map(lambda _: VMEM, out_shape)
    return pl.pallas_call(
        body,
        out_shape=out_shape,
        in_specs=in_specs,
        out_specs=out_specs,
        scratch_shapes=scratch,
        input_output_aliases=aliases or {},
        compiler_params=pltpu.CompilerParams(vmem_limit_bytes=12 << 20),
        cost_estimate=pl.CostEstimate(flops=1<<33, bytes_accessed=1<<25, transcendentals=0),
    )(*args)


def array(shape, dtype):
    return jax.ShapeDtypeStruct(shape, dtype)


def one(scalar):
    return scalar.reshape(1)


def multiply(piece, w_parts, first=None):
    parts = len(w_parts)

    def body(*refs):
        if first is None:
            refs = (None, *refs)
        piece_ref, ws, outs = refs[1], refs[2 : 2 + parts], refs[2 + parts :]

        def work(order):
            for k in range(parts):
                outs[k][...] = dot_last(piece_ref[...], ws[order[k]][...]).astype(BF16)

        if first is None:
            work(range(parts))
        else:
            pl.when(refs[0][0] == 0)(lambda: work((0, 1)))
            pl.when(refs[0][0] == 1)(lambda: work((1, 0)))

    shapes = [array((piece.shape[0], w.shape[0]), BF16) for w in w_parts]
    head = [] if first is None else [first]
    return list(call(body, shapes, [*head, piece, *w_parts], {i: SMEM for i in range(len(head))}))


def project(core, ids, x, g, down_t, up_t, rank):
    adapters = down_t.shape[0] // rank

    def body(core_ref, ids_ref, x_ref, g_ref, down_ref, up_ref, out_ref):
        own_ids = ids_ref[pl.ds(core_ref[0], 1), :]
        for i, (rows, factors) in enumerate(((x_ref, down_ref), (g_ref, up_ref))):
            every = dot_last(factors[...], rows[...])
            own = jnp.zeros((rank, every.shape[1]), F32)
            for a in range(adapters):
                own += jnp.where(own_ids == a, every[a * rank : (a + 1) * rank], 0.0)
            out_ref[i * rank : (i + 1) * rank] = own

    shape = array((2 * rank, x.shape[0]), F32)
    return call(body, shape, [core, ids, x, g, down_t, up_t], {0: SMEM})


def slot_row(ids, slot_ref, adapters):
    slot = jnp.zeros(ids.shape, jnp.int32)
    for a in range(adapters):
        slot = jnp.where(ids == a, slot_ref[a], slot)
    return slot


def lift_down(owner_slot, core, ids, x, lows, slots):
    adapters, cores = owner_slot.shape[0], ids.shape[0]
    rank = lows[0].shape[0] // 2
    rows, width = x.shape
    half = width // 2

    def body(slot_ref, core_ref, ids_ref, x_ref, *rest):
        low_refs = rest[: len(lows)]
        card_ref, low_ref, mine_ref, away_ref, spread_ref = rest[len(lows) :]
        low = low_refs[0][...]
        for ref in low_refs[1:]:
            low = low + ref[...]
        card_ref[...] = jnp.concatenate(
            [
                low[:rank],
                ids_ref[...].astype(F32),
                jnp.zeros((OWN_MAX * rank - rank - cores, rows), F32),
            ],
            axis=0,
        ).astype(BF16)
        low_out = low[rank:].astype(BF16)
        low_ref[...] = low_out
        core = core_ref[0]
        slot = slot_row(ids_ref[pl.ds(core, 1), :], slot_ref, adapters)
        for s in range(slots):
            part = jnp.where(slot == s, low_out.astype(F32), 0.0)
            spread_ref[s * rank : (s + 1) * rank] = part.astype(BF16)
        for ref, part in ((mine_ref, core), (away_ref, 1 - core)):
            at = pl.ds(pl.multiple_of(part * half, 128), half)
            ref[...] = dot_plain(spread_ref[...], x_ref[:, at]).astype(BF16)

    wide = array((slots * rank, half), BF16)
    shapes = [array((OWN_MAX * rank, rows), BF16), array((rank, rows), BF16), wide, wide]
    scratch = [pltpu.VMEM((slots * rank, rows), BF16)]
    args = [owner_slot, core, ids, x, *lows]
    return call(body, shapes, args, {0: SMEM, 1: SMEM}, scratch=scratch)


def letters(place, card, mine, got, n):
    deep, half, rows = mine.shape[0] // n, mine.shape[1], card.shape[1]

    def body(place_ref, card_ref, mine_ref, got_ref, *outs):
        for s, out in enumerate(outs):
            at = pl.ds(pl.multiple_of((place_ref[0] ^ s) * deep, 16), deep)
            total = mine_ref[at].astype(F32) + got_ref[at].astype(F32)
            out[:, :half] = total.astype(BF16)
            out[:, half:] = card_ref[...]

    shapes = [array((deep, half + rows), BF16)] * n
    return call(body, shapes, [place, card, mine, got], {0: SMEM})


def lift_up(owner_slot, core, place, cards, blocks, rank):
    n, adapters = len(blocks), owner_slot.shape[0]
    width = blocks[0].shape[1]
    half = width // 2

    def body(slot_ref, core_ref, place_ref, *refs):
        card_refs, block_refs, outs = refs[:n], refs[n : 2 * n], refs[2 * n :]
        core, first = core_ref[0], place_ref[0] * OWN_MAX
        lifts = []
        for ref in card_refs:
            card = ref[...].astype(F32)
            ids = jnp.where(core == 0, card[rank : rank + 1], card[rank + 1 : rank + 2])
            slot = slot_row(ids.astype(jnp.int32), slot_ref, adapters)
            lift = [jnp.where(slot == first + o, card[:rank], 0.0) for o in range(OWN_MAX)]
            lifts.append(jnp.concatenate(lift, axis=0).astype(BF16))
        if half % 128:
            outs[0][...] = sum(dot_plain(a, b[...]) for a, b in zip(lifts, block_refs))
            return
        for ref, part in zip(outs, (core, 1 - core)):
            at = pl.ds(pl.multiple_of(part * half, 128), half)
            ref[...] = sum(dot_plain(a, b[:, at]) for a, b in zip(lifts, block_refs))

    deep = OWN_MAX * rank
    shapes = [array((deep, width), F32)] if half % 128 else [array((deep, half), F32)] * 2
    args = [owner_slot, core, place, *cards, *blocks]
    out = call(body, shapes, args, {0: SMEM, 1: SMEM, 2: SMEM})
    if half % 128:
        at = core[0] * half
        return [lax.dynamic_slice_in_dim(out[0], p, half, 1) for p in (at, half - at)]
    return out


def finish(weight, core, offsets, ids, low_out, down_t, pieces, into=None):
    rows, width = ids.shape[1], down_t.shape[1]
    rank = low_out.shape[0]
    adapters, chunk, count = weight.shape[0], pieces[0].shape[1], len(pieces)

    def body(weight_ref, core_ref, *refs):
        offset_refs, (ids_ref, low_ref, down_ref) = refs[:count], refs[count : count + 3]
        piece_refs, (out_ref, held, sems) = refs[count + 3 : 2 * count + 3], refs[-3:]
        own_ids = ids_ref[pl.ds(core_ref[0], 1), :]
        scale = jnp.zeros(own_ids.shape, F32)
        spread = []
        for a in range(adapters):
            scale = jnp.where(own_ids == a, weight_ref[a], scale)
            spread.append(jnp.where(own_ids == a, low_ref[...].astype(F32), 0.0))
        spread = jnp.concatenate(spread, axis=0).astype(BF16)
        scale = jnp.broadcast_to(scale, (rows, rows)).T[:, :1]
        copies = []
        for i in range(count):
            at = pl.ds(pl.multiple_of(offset_refs[i][0], 128), chunk)
            term = dot_first(spread, down_ref[:, at])
            total = piece_refs[i][...].astype(F32) + ADAPTER_SCALE * term
            held[i] = (scale * total).astype(BF16)
            copies.append(pltpu.make_async_copy(held.at[i], out_ref.at[:, at], sems.at[i]))
            copies[-1].start()
        for copy in copies:
            copy.wait()

    args = [weight, core, *offsets, ids, low_out, down_t, *pieces]
    specs = {i: SMEM for i in range(2 + count)}
    aliases = None
    if into is not None:
        specs[len(args)] = ANY
        aliases = {len(args): 0}
        args.append(into)
    scratch = [pltpu.VMEM((count, rows, chunk), BF16), pltpu.SemaphoreType.DMA((count,))]
    shape = array((rows, width), BF16)
    return call(body, shape, args, specs, out_specs=ANY, scratch=scratch, aliases=aliases)


def swap(value, axis, step):
    size = lax.axis_size(axis)
    return lax.ppermute(value, axis, [(i, i ^ step) for i in range(size)])


def pick(value, index):
    return lax.dynamic_index_in_dim(value, index, 0, keepdims=False)


def choose(values, index):
    out = values[0]
    for i in range(1, len(values)):
        out = jnp.where(index == i, values[i], out)
    return out


def after(value, *others):
    return lax.optimization_barrier((value, *others))[0]


def local(x, g, ids, owner_slot, w, down, up):
    rows = x.shape[0]
    adapters = owner_slot.shape[0]
    rank = up.shape[1]
    n, tensors, cores = lax.axis_size("dp"), lax.axis_size("tensor"), lax.axis_size("seq")
    z, t, c = lax.axis_index("dp"), lax.axis_index("tensor"), lax.axis_index("seq")
    core, place = one(c), one(z)
    slots = n * OWN_MAX
    labels = jnp.arange(adapters, dtype=jnp.int32)
    ids = ids.reshape(cores, rows)

    top = n // 2
    blocks = {0: g, top: swap(g, "dp", top)}

    def hand_on(froms, *ready):
        bit = top // 2
        while bit:
            for s in [s for s in blocks if s in froms]:
                blocks[s ^ bit] = swap(after(blocks[s], *ready), "dp", bit)
            bit //= 2

    hand_on(range(top))

    w_other = swap(w, "seq", 1)
    width = cores * w.shape[0]
    chunk = width // tensors
    first = None
    if tensors == cores:
        w_parts, first = [w, w_other], one(t ^ c)
    else:
        w_chip = jnp.where(c == 0, jnp.stack([w, w_other]), jnp.stack([w_other, w]))
        w_chip = w_chip.reshape(tensors, chunk, -1)
        w_parts = [pick(w_chip, t ^ k) for k in range(tensors)]

    parts, totals = [], []

    def product(s, *ready):
        made = multiply(after(blocks[s], *ready), w_parts, first)
        kept = made[0].astype(F32)
        for k in range(1, tensors):
            kept = kept + swap(made[k], "tensor", k).astype(F32)
        parts.append(made)
        totals.append(kept.astype(BF16))

    product(0)

    down_t = down.transpose(1, 2, 0).reshape(adapters * rank, -1)
    up_t = up.reshape(adapters * rank, -1)
    low = project(core, after(ids, *parts[0]), x, g, down_t, up_t, rank)
    lows = [low] + [swap(low, "tensor", s) for s in range(1, tensors)]

    product(1, low)
    card, low_out, mine, away = lift_down(
        owner_slot, core, after(ids, *parts[1]), x, lows, slots
    )
    got = swap(away, "seq", 1)

    hand_on(range(top, n), mine)
    for s in range(2, n - 1):
        product(s, *parts[s - 1], mine, away)

    sent = letters(place, card, mine, after(got, *parts[n - 2]), n)

    product(n - 1, *parts[n - 2])

    received = [sent[0]] + [swap(sent[s], "dp", s) for s in range(1, n)]
    half = mine.shape[1]
    cards = [v[:, half:] for v in received]
    down_sum = sum(v[:, :half].astype(F32) for v in received)
    all_ids = jnp.stack([v[rank : rank + cores] for v in cards]).astype(jnp.int32)
    counts = jnp.sum((all_ids.reshape(1, -1) == labels[:, None]).astype(F32), axis=1)
    weight = F32(n * cores * rows) / (F32(adapters) * counts)
    my_slots = z * OWN_MAX + jnp.arange(OWN_MAX, dtype=jnp.int32)
    slot_weight = ADAPTER_SCALE * jnp.sum(
        jnp.where(owner_slot[None, :] == my_slots[:, None], weight[None, :], 0.0), axis=1
    )
    down_grad = down_sum.reshape(OWN_MAX, rank, half) * slot_weight[:, None, None]
    down_grad = down_grad.transpose(2, 0, 1)

    back = [swap(v, "dp", s) if s else v for s, v in enumerate(totals)]
    span = n // tensors
    low_bits, high_bits = z % span, z // span
    pieces, offsets = [], []
    for r in range(span):
        choices = [back[r + k * span] for k in range(tensors)]
        choices[0] = after(choices[0], *parts[n - 1])
        for k in range(tensors):
            piece = choose(choices, t ^ k ^ high_bits)
            pieces.append(swap(piece, "tensor", k) if k else piece)
            offsets.append((r ^ low_bits) * width + (t ^ k) * chunk)
    if chunk % 128 == 0:
        offsets = [one(v) for v in offsets]
        args = (ids, low_out, down_t)
        early = finish(weight, core, offsets[:-1], *args, pieces[:-1])
        input_gradient = finish(weight, core, offsets[-1:], *args, pieces[-1:], into=early)
    else:
        base = jnp.zeros((rows, span * width), BF16)
        for piece, offset in zip(pieces, offsets):
            base = lax.dynamic_update_slice_in_dim(base, piece, offset, 1)
        own_match = (pick(ids, c)[:, None] == labels[None, :]).astype(F32)
        own_weight = jnp.sum(own_match * weight[None, :], axis=1)
        spread = (own_match.T.astype(BF16)[:, None, :] * low_out[None]).reshape(-1, rows)
        total = base.astype(F32) + ADAPTER_SCALE * dot_first(spread, down_t)
        input_gradient = (own_weight[:, None] * total).astype(BF16)

    up_mine, up_away = lift_up(
        owner_slot, core, place, cards, [blocks[s] for s in range(n)], rank
    )
    up_sum = up_mine + swap(up_away, "seq", 1)
    up_grad = up_sum.reshape(OWN_MAX, rank, -1) * slot_weight[:, None, None]
    return input_gradient, down_grad, up_grad


def solution(mesh):
    in_specs = (
        P(("groups", "dp", "seq"), "tensor"),
        P(("groups", "dp", "seq"), "tensor"),
        P(("groups", "dp")),
        P("groups"),
        P(("dp", "seq"), "tensor"),
        P(("groups", "tensor"), None, None),
        P("groups", None, "tensor"),
    )
    out_specs = (
        P(("groups", "dp", "seq"), "tensor"),
        P(("groups", "tensor", "seq"), "dp", None),
        P(("groups", "dp"), None, ("tensor", "seq")),
    )
    return jax.shard_map(local, mesh=mesh, in_specs=in_specs, out_specs=out_specs, check_vma=False)
```

```python
import jax
import jax.numpy as jnp
from jax import lax
from jax.experimental import pallas as pl
from jax.experimental.pallas import tpu as pltpu
from jax.sharding import PartitionSpec as P

OWN_MAX = 2
ADAPTER_SCALE = 2.0
F32 = jnp.float32
BF16 = jnp.bfloat16
VMEM = pl.BlockSpec(memory_space=pltpu.VMEM)
SMEM = pl.BlockSpec(memory_space=pltpu.SMEM)
ANY = pl.BlockSpec(memory_space=pl.ANY)


def dot_last(left, right):
    return lax.dot_general(left, right, (((1,), (1,)), ((), ())), preferred_element_type=F32)


def dot_plain(left, right):
    return lax.dot_general(left, right, (((1,), (0,)), ((), ())), preferred_element_type=F32)


def dot_first(left, right):
    return lax.dot_general(left, right, (((0,), (0,)), ((), ())), preferred_element_type=F32)


def call(body, out_shape, args, specs, out_specs=None, scratch=(), aliases=None):
    in_specs = [specs.get(i, VMEM) for i in range(len(args))]
    if out_specs is None:
        out_specs = jax.tree.map(lambda _: VMEM, out_shape)
    return pl.pallas_call(
        body,
        out_shape=out_shape,
        in_specs=in_specs,
        out_specs=out_specs,
        scratch_shapes=scratch,
        input_output_aliases=aliases or {},
        compiler_params=pltpu.CompilerParams(vmem_limit_bytes=12 << 20),
        cost_estimate=pl.CostEstimate(flops=1<<33, bytes_accessed=1<<25, transcendentals=0),
    )(*args)


def array(shape, dtype):
    return jax.ShapeDtypeStruct(shape, dtype)


def one(scalar):
    return scalar.reshape(1)


def multiply(piece, w_parts, first=None):
    parts = len(w_parts)

    def body(*refs):
        if first is None:
            refs = (None, *refs)
        piece_ref, ws, outs = refs[1], refs[2 : 2 + parts], refs[2 + parts :]

        def work(order):
            for k in range(parts):
                outs[k][...] = dot_last(piece_ref[...], ws[order[k]][...]).astype(BF16)

        if first is None:
            work(range(parts))
        else:
            pl.when(refs[0][0] == 0)(lambda: work((0, 1)))
            pl.when(refs[0][0] == 1)(lambda: work((1, 0)))

    shapes = [array((piece.shape[0], w.shape[0]), BF16) for w in w_parts]
    head = [] if first is None else [first]
    return list(call(body, shapes, [*head, piece, *w_parts], {i: SMEM for i in range(len(head))}))


def project(core, ids, x, g, down_t, up_t, rank):
    adapters = down_t.shape[0] // rank

    def body(core_ref, ids_ref, x_ref, g_ref, down_ref, up_ref, out_ref):
        own_ids = ids_ref[pl.ds(core_ref[0], 1), :]
        for i, (rows, factors) in enumerate(((x_ref, down_ref), (g_ref, up_ref))):
            every = dot_last(factors[...], rows[...])
            own = jnp.zeros((rank, every.shape[1]), F32)
            for a in range(adapters):
                own += jnp.where(own_ids == a, every[a * rank : (a + 1) * rank], 0.0)
            out_ref[i * rank : (i + 1) * rank] = own

    shape = array((2 * rank, x.shape[0]), F32)
    return call(body, shape, [core, ids, x, g, down_t, up_t], {0: SMEM})


def slot_row(ids, slot_ref, adapters):
    slot = jnp.zeros(ids.shape, jnp.int32)
    for a in range(adapters):
        slot = jnp.where(ids == a, slot_ref[a], slot)
    return slot


def lift_down(owner_slot, core, ids, x, lows, slots):
    adapters, cores = owner_slot.shape[0], ids.shape[0]
    rank = lows[0].shape[0] // 2
    rows, width = x.shape
    half = width // 2

    def body(slot_ref, core_ref, ids_ref, x_ref, *rest):
        low_refs = rest[: len(lows)]
        card_ref, low_ref, mine_ref, away_ref, spread_ref = rest[len(lows) :]
        low = low_refs[0][...]
        for ref in low_refs[1:]:
            low = low + ref[...]
        card_ref[...] = jnp.concatenate(
            [
                low[:rank],
                ids_ref[...].astype(F32),
                jnp.zeros((OWN_MAX * rank - rank - cores, rows), F32),
            ],
            axis=0,
        ).astype(BF16)
        low_out = low[rank:].astype(BF16)
        low_ref[...] = low_out
        core = core_ref[0]
        slot = slot_row(ids_ref[pl.ds(core, 1), :], slot_ref, adapters)
        for s in range(slots):
            part = jnp.where(slot == s, low_out.astype(F32), 0.0)
            spread_ref[s * rank : (s + 1) * rank] = part.astype(BF16)
        for ref, part in ((mine_ref, core), (away_ref, 1 - core)):
            at = pl.ds(pl.multiple_of(part * half, 128), half)
            ref[...] = dot_plain(spread_ref[...], x_ref[:, at]).astype(BF16)

    wide = array((slots * rank, half), BF16)
    shapes = [array((OWN_MAX * rank, rows), BF16), array((rank, rows), BF16), wide, wide]
    scratch = [pltpu.VMEM((slots * rank, rows), BF16)]
    args = [owner_slot, core, ids, x, *lows]
    return call(body, shapes, args, {0: SMEM, 1: SMEM}, scratch=scratch)


def chip_sums(place, card, mine, got, n):
    deep, half, rows = mine.shape[0] // n, mine.shape[1], card.shape[1]
    top = n // 2

    def body(place_ref, card_ref, mine_ref, got_ref, *outs):
        for s in range(n):
            at = pl.ds(pl.multiple_of((place_ref[0] ^ s) * deep, 16), deep)
            total = (mine_ref[at].astype(F32) + got_ref[at].astype(F32)).astype(BF16)
            if s < top:
                outs[s][...] = total
            else:
                outs[top][:, (s - top) * half : (s - top + 1) * half] = total
        outs[top][:, top * half :] = card_ref[...]

    shapes = [array((deep, half), BF16)] * top + [array((deep, top * half + rows), BF16)]
    return list(call(body, shapes, [place, card, mine, got], {0: SMEM}))


def lift_up(owner_slot, core, place, cards, blocks, rank):
    n, adapters = len(blocks), owner_slot.shape[0]
    width = blocks[0].shape[1]
    half = width // 2

    def body(slot_ref, core_ref, place_ref, *refs):
        card_refs, block_refs, outs = refs[:n], refs[n : 2 * n], refs[2 * n :]
        core, first = core_ref[0], place_ref[0] * OWN_MAX
        lifts = []
        for ref in card_refs:
            card = ref[...].astype(F32)
            ids = jnp.where(core == 0, card[rank : rank + 1], card[rank + 1 : rank + 2])
            slot = slot_row(ids.astype(jnp.int32), slot_ref, adapters)
            lift = [jnp.where(slot == first + o, card[:rank], 0.0) for o in range(OWN_MAX)]
            lifts.append(jnp.concatenate(lift, axis=0).astype(BF16))
        if half % 128:
            outs[0][...] = sum(dot_plain(a, b[...]) for a, b in zip(lifts, block_refs))
            return
        for ref, part in zip(outs, (core, 1 - core)):
            at = pl.ds(pl.multiple_of(part * half, 128), half)
            ref[...] = sum(dot_plain(a, b[:, at]) for a, b in zip(lifts, block_refs))

    deep = OWN_MAX * rank
    shapes = [array((deep, width), F32)] if half % 128 else [array((deep, half), F32)] * 2
    args = [owner_slot, core, place, *cards, *blocks]
    out = call(body, shapes, args, {0: SMEM, 1: SMEM, 2: SMEM})
    if half % 128:
        at = core[0] * half
        return [lax.dynamic_slice_in_dim(out[0], p, half, 1) for p in (at, half - at)]
    return out


def finish(weight, core, offsets, ids, low_out, down_t, pieces, into=None):
    rows, width = ids.shape[1], down_t.shape[1]
    rank = low_out.shape[0]
    adapters, chunk, count = weight.shape[0], pieces[0].shape[1], len(pieces)

    def body(weight_ref, core_ref, *refs):
        offset_refs, (ids_ref, low_ref, down_ref) = refs[:count], refs[count : count + 3]
        piece_refs, (out_ref, held, sems) = refs[count + 3 : 2 * count + 3], refs[-3:]
        own_ids = ids_ref[pl.ds(core_ref[0], 1), :]
        scale = jnp.zeros(own_ids.shape, F32)
        spread = []
        for a in range(adapters):
            scale = jnp.where(own_ids == a, weight_ref[a], scale)
            spread.append(jnp.where(own_ids == a, low_ref[...].astype(F32), 0.0))
        spread = jnp.concatenate(spread, axis=0).astype(BF16)
        scale = jnp.broadcast_to(scale, (rows, rows)).T[:, :1]
        copies = []
        for i in range(count):
            at = pl.ds(pl.multiple_of(offset_refs[i][0], 128), chunk)
            term = dot_first(spread, down_ref[:, at])
            total = piece_refs[i][...].astype(F32) + ADAPTER_SCALE * term
            held[i] = (scale * total).astype(BF16)
            copies.append(pltpu.make_async_copy(held.at[i], out_ref.at[:, at], sems.at[i]))
            copies[-1].start()
        for copy in copies:
            copy.wait()

    args = [weight, core, *offsets, ids, low_out, down_t, *pieces]
    specs = {i: SMEM for i in range(2 + count)}
    aliases = None
    if into is not None:
        specs[len(args)] = ANY
        aliases = {len(args): 0}
        args.append(into)
    scratch = [pltpu.VMEM((count, rows, chunk), BF16), pltpu.SemaphoreType.DMA((count,))]
    shape = array((rows, width), BF16)
    return call(body, shape, args, specs, out_specs=ANY, scratch=scratch, aliases=aliases)


def swap(value, axis, step):
    size = lax.axis_size(axis)
    return lax.ppermute(value, axis, [(i, i ^ step) for i in range(size)])


def pick(value, index):
    return lax.dynamic_index_in_dim(value, index, 0, keepdims=False)


def choose(values, index):
    out = values[0]
    for i in range(1, len(values)):
        out = jnp.where(index == i, values[i], out)
    return out


def after(value, *others):
    return lax.optimization_barrier((value, *others))[0]


def local(x, g, ids, owner_slot, w, down, up):
    rows = x.shape[0]
    adapters = owner_slot.shape[0]
    rank = up.shape[1]
    n, tensors, cores = lax.axis_size("dp"), lax.axis_size("tensor"), lax.axis_size("seq")
    z, t, c = lax.axis_index("dp"), lax.axis_index("tensor"), lax.axis_index("seq")
    core, place = one(c), one(z)
    slots = n * OWN_MAX
    labels = jnp.arange(adapters, dtype=jnp.int32)
    ids = ids.reshape(cores, rows)

    top = n // 2
    blocks = {0: g, top: swap(g, "dp", top)}

    def hand_on(froms, *ready):
        bit = top // 2
        while bit:
            for s in [s for s in blocks if s in froms]:
                blocks[s ^ bit] = swap(after(blocks[s], *ready), "dp", bit)
            bit //= 2

    hand_on(range(top))

    w_other = swap(w, "seq", 1)
    width = cores * w.shape[0]
    chunk = width // tensors
    first = None
    if tensors == cores:
        w_parts, first = [w, w_other], one(t ^ c)
    else:
        w_chip = jnp.where(c == 0, jnp.stack([w, w_other]), jnp.stack([w_other, w]))
        w_chip = w_chip.reshape(tensors, chunk, -1)
        w_parts = [pick(w_chip, t ^ k) for k in range(tensors)]

    parts, totals = {}, {}

    def product(s, *ready):
        made = multiply(after(blocks[s], *ready), w_parts, first)
        kept = made[0].astype(F32)
        for k in range(1, tensors):
            kept = kept + swap(made[k], "tensor", k).astype(F32)
        parts[s], totals[s] = made, kept.astype(BF16)

    down_t = down.transpose(1, 2, 0).reshape(adapters * rank, -1)
    up_t = up.reshape(adapters * rank, -1)
    low = project(core, after(ids, w_other), x, g, down_t, up_t, rank)
    lows = [low] + [swap(low, "tensor", s) for s in range(1, tensors)]

    product(0, low)
    card, low_out, mine, away = lift_down(owner_slot, core, ids, x, lows, slots)
    half = mine.shape[1]
    got = swap(after(away, blocks[top]), "seq", 1)
    *held, letter = chip_sums(place, card, mine, got, n)
    cards = {0: card}

    def post(bit, letter):
        known = list(cards)
        got = swap(letter, "dp", bit)
        for s in range(bit):
            total = held[s].astype(F32) + got[:, s * half : (s + 1) * half].astype(F32)
            held[s] = total.astype(BF16) if bit > 1 else total
        for i, s in enumerate(known):
            at = bit * half + i * rows
            cards[s ^ bit] = got[:, at : at + rows]

    post(top, letter)
    hand_on(range(top, n), low, *parts[0])
    order = [*range(top, n - 1), *range(1, top)]
    ready = [letter]
    for s in order:
        product(s, *ready)
        ready = parts[s]
    product(n - 1, *ready, totals[order[0]])
    bit = top // 2
    while bit:
        letter = held[bit : 2 * bit] + [cards[s] for s in cards]
        post(bit, after(jnp.concatenate(letter, axis=1), totals[n - 1]))
        bit //= 2
    cards = [after(cards[s], totals[n - 1]) for s in range(n)]
    down_sum = after(held[0], totals[n - 1])
    all_ids = jnp.stack([v[rank : rank + cores] for v in cards]).astype(jnp.int32)
    counts = jnp.sum((all_ids.reshape(1, -1) == labels[:, None]).astype(F32), axis=1)
    weight = F32(n * cores * rows) / (F32(adapters) * counts)
    my_slots = z * OWN_MAX + jnp.arange(OWN_MAX, dtype=jnp.int32)
    slot_weight = ADAPTER_SCALE * jnp.sum(
        jnp.where(owner_slot[None, :] == my_slots[:, None], weight[None, :], 0.0), axis=1
    )
    down_grad = down_sum.reshape(OWN_MAX, rank, half) * slot_weight[:, None, None]
    down_grad = down_grad.transpose(2, 0, 1)

    back = [swap(v, "dp", s) if s else v for s, v in sorted(totals.items())]
    span = n // tensors
    low_bits, high_bits = z % span, z // span
    pieces, offsets = [], []
    for r in range(span):
        choices = [back[r + k * span] for k in range(tensors)]
        choices[0] = after(choices[0], totals[n - 1])
        for k in range(tensors):
            piece = choose(choices, t ^ k ^ high_bits)
            pieces.append(swap(piece, "tensor", k) if k else piece)
            offsets.append((r ^ low_bits) * width + (t ^ k) * chunk)
    if chunk % 128 == 0:
        offsets = [one(v) for v in offsets]
        args = (ids, low_out, down_t)
        early = finish(weight, core, offsets[:-1], *args, pieces[:-1])
        input_gradient = finish(weight, core, offsets[-1:], *args, pieces[-1:], into=early)
    else:
        base = jnp.zeros((rows, span * width), BF16)
        for piece, offset in zip(pieces, offsets):
            base = lax.dynamic_update_slice_in_dim(base, piece, offset, 1)
        own_match = (pick(ids, c)[:, None] == labels[None, :]).astype(F32)
        own_weight = jnp.sum(own_match * weight[None, :], axis=1)
        spread = (own_match.T.astype(BF16)[:, None, :] * low_out[None]).reshape(-1, rows)
        total = base.astype(F32) + ADAPTER_SCALE * dot_first(spread, down_t)
        input_gradient = (own_weight[:, None] * total).astype(BF16)

    up_mine, up_away = lift_up(
        owner_slot, core, place, cards, [blocks[s] for s in range(n)], rank
    )
    up_sum = up_mine + swap(up_away, "seq", 1)
    up_grad = up_sum.reshape(OWN_MAX, rank, -1) * slot_weight[:, None, None]
    return input_gradient, down_grad, up_grad


def solution(mesh):
    in_specs = (
        P(("groups", "dp", "seq"), "tensor"),
        P(("groups", "dp", "seq"), "tensor"),
        P(("groups", "dp")),
        P("groups"),
        P(("dp", "seq"), "tensor"),
        P(("groups", "tensor"), None, None),
        P("groups", None, "tensor"),
    )
    out_specs = (
        P(("groups", "dp", "seq"), "tensor"),
        P(("groups", "tensor", "seq"), "dp", None),
        P(("groups", "dp"), None, ("tensor", "seq")),
    )
    return jax.shard_map(local, mesh=mesh, in_specs=in_specs, out_specs=out_specs, check_vma=False)
```

```python
import jax
import jax.numpy as jnp
from jax import lax
from jax.experimental import pallas as pl
from jax.experimental.pallas import tpu as pltpu
from jax.sharding import PartitionSpec as P

OWN_MAX = 2
CUTS = 2
ADAPTER_SCALE = 2.0
F32 = jnp.float32
BF16 = jnp.bfloat16
VMEM = pl.BlockSpec(memory_space=pltpu.VMEM)
SMEM = pl.BlockSpec(memory_space=pltpu.SMEM)
ANY = pl.BlockSpec(memory_space=pl.ANY)


def dot_last(left, right):
    return lax.dot_general(left, right, (((1,), (1,)), ((), ())), preferred_element_type=F32)


def dot_plain(left, right):
    return lax.dot_general(left, right, (((1,), (0,)), ((), ())), preferred_element_type=F32)


def dot_first(left, right):
    return lax.dot_general(left, right, (((0,), (0,)), ((), ())), preferred_element_type=F32)


def call(body, out_shape, args, specs, out_specs=None, scratch=(), aliases=None):
    in_specs = [specs.get(i, VMEM) for i in range(len(args))]
    if out_specs is None:
        out_specs = jax.tree.map(lambda _: VMEM, out_shape)
    return pl.pallas_call(
        body,
        out_shape=out_shape,
        in_specs=in_specs,
        out_specs=out_specs,
        scratch_shapes=scratch,
        input_output_aliases=aliases or {},
        compiler_params=pltpu.CompilerParams(vmem_limit_bytes=12 << 20),
        cost_estimate=pl.CostEstimate(flops=1<<33, bytes_accessed=1<<25, transcendentals=0),
    )(*args)


def array(shape, dtype):
    return jax.ShapeDtypeStruct(shape, dtype)


def one(scalar):
    return scalar.reshape(1)


def multiply(piece, w_parts, first=None, chosen=None, cuts=1):
    parts = len(w_parts)
    chosen = range(parts) if chosen is None else chosen
    rows = piece.shape[0] // cuts

    def body(*refs):
        if first is None:
            refs = (None, *refs)
        piece_ref, ws, outs = refs[1], refs[2 : 2 + parts], refs[2 + parts :]

        def work(order):
            for i, k in enumerate(chosen):
                value = dot_last(piece_ref[...], ws[order[k]][...]).astype(BF16)
                for j in range(cuts):
                    outs[i * cuts + j][...] = value[j * rows : (j + 1) * rows]

        if first is None:
            work(range(parts))
        else:
            pl.when(refs[0][0] == 0)(lambda: work((0, 1)))
            pl.when(refs[0][0] == 1)(lambda: work((1, 0)))

    shapes = [array((rows, w_parts[k].shape[0]), BF16) for k in chosen for _ in range(cuts)]
    head = [] if first is None else [first]
    return list(call(body, shapes, [*head, piece, *w_parts], {i: SMEM for i in range(len(head))}))


def project(core, ids, x, g, down_t, up_t, rank):
    adapters = down_t.shape[0] // rank

    def body(core_ref, ids_ref, x_ref, g_ref, down_ref, up_ref, out_ref):
        own_ids = ids_ref[pl.ds(core_ref[0], 1), :]
        for i, (rows, factors) in enumerate(((x_ref, down_ref), (g_ref, up_ref))):
            every = dot_last(factors[...], rows[...])
            own = jnp.zeros((rank, every.shape[1]), F32)
            for a in range(adapters):
                own += jnp.where(own_ids == a, every[a * rank : (a + 1) * rank], 0.0)
            out_ref[i * rank : (i + 1) * rank] = own

    shape = array((2 * rank, x.shape[0]), F32)
    return call(body, shape, [core, ids, x, g, down_t, up_t], {0: SMEM})


def slot_row(ids, slot_ref, adapters):
    slot = jnp.zeros(ids.shape, jnp.int32)
    for a in range(adapters):
        slot = jnp.where(ids == a, slot_ref[a], slot)
    return slot


def lift_down(owner_slot, core, ids, x, lows, slots):
    adapters, cores = owner_slot.shape[0], ids.shape[0]
    rank = lows[0].shape[0] // 2
    rows, width = x.shape
    half = width // 2

    def body(slot_ref, core_ref, ids_ref, x_ref, *rest):
        low_refs = rest[: len(lows)]
        card_ref, low_ref, mine_ref, away_ref, spread_ref = rest[len(lows) :]
        low = low_refs[0][...]
        for ref in low_refs[1:]:
            low = low + ref[...]
        card_ref[...] = jnp.concatenate(
            [
                low[:rank],
                ids_ref[...].astype(F32),
                jnp.zeros((OWN_MAX * rank - rank - cores, rows), F32),
            ],
            axis=0,
        ).astype(BF16)
        low_out = low[rank:].astype(BF16)
        low_ref[...] = low_out
        core = core_ref[0]
        slot = slot_row(ids_ref[pl.ds(core, 1), :], slot_ref, adapters)
        for s in range(slots):
            part = jnp.where(slot == s, low_out.astype(F32), 0.0)
            spread_ref[s * rank : (s + 1) * rank] = part.astype(BF16)
        for ref, part in ((mine_ref, core), (away_ref, 1 - core)):
            at = pl.ds(pl.multiple_of(part * half, 128), half)
            ref[...] = dot_plain(spread_ref[...], x_ref[:, at]).astype(BF16)

    wide = array((slots * rank, half), BF16)
    shapes = [array((OWN_MAX * rank, rows), BF16), array((rank, rows), BF16), wide, wide]
    scratch = [pltpu.VMEM((slots * rank, rows), BF16)]
    args = [owner_slot, core, ids, x, *lows]
    return call(body, shapes, args, {0: SMEM, 1: SMEM}, scratch=scratch)


def chip_sums(place, card, mine, got, n):
    deep, half, rows = mine.shape[0] // n, mine.shape[1], card.shape[1]
    top = n // 2

    def body(place_ref, card_ref, mine_ref, got_ref, *outs):
        for s in range(n):
            at = pl.ds(pl.multiple_of((place_ref[0] ^ s) * deep, 16), deep)
            total = (mine_ref[at].astype(F32) + got_ref[at].astype(F32)).astype(BF16)
            if s < top:
                outs[s][...] = total
            else:
                outs[top][:, (s - top) * half : (s - top + 1) * half] = total
        outs[top][:, top * half :] = card_ref[...]

    shapes = [array((deep, half), BF16)] * top + [array((deep, top * half + rows), BF16)]
    return list(call(body, shapes, [place, card, mine, got], {0: SMEM}))


def lift_up(owner_slot, core, place, cards, blocks, rank):
    n, adapters = len(blocks), owner_slot.shape[0]
    width = blocks[0].shape[1]
    half = width // 2

    def body(slot_ref, core_ref, place_ref, *refs):
        card_refs, block_refs, outs = refs[:n], refs[n : 2 * n], refs[2 * n :]
        core, first = core_ref[0], place_ref[0] * OWN_MAX
        lifts = []
        for ref in card_refs:
            card = ref[...].astype(F32)
            ids = jnp.where(core == 0, card[rank : rank + 1], card[rank + 1 : rank + 2])
            slot = slot_row(ids.astype(jnp.int32), slot_ref, adapters)
            lift = [jnp.where(slot == first + o, card[:rank], 0.0) for o in range(OWN_MAX)]
            lifts.append(jnp.concatenate(lift, axis=0).astype(BF16))
        if half % 128:
            outs[0][...] = sum(dot_plain(a, b[...]) for a, b in zip(lifts, block_refs))
            return
        for ref, part in zip(outs, (core, 1 - core)):
            at = pl.ds(pl.multiple_of(part * half, 128), half)
            ref[...] = sum(dot_plain(a, b[:, at]) for a, b in zip(lifts, block_refs))

    deep = OWN_MAX * rank
    shapes = [array((deep, width), F32)] if half % 128 else [array((deep, half), F32)] * 2
    args = [owner_slot, core, place, *cards, *blocks]
    out = call(body, shapes, args, {0: SMEM, 1: SMEM, 2: SMEM})
    if half % 128:
        at = core[0] * half
        return [lax.dynamic_slice_in_dim(out[0], p, half, 1) for p in (at, half - at)]
    return out


def finish(weight, core, ids, low_out, down_t, pieces, offsets, starts, into=None):
    rows, width = ids.shape[1], down_t.shape[1]
    rank = low_out.shape[0]
    adapters, count = weight.shape[0], len(pieces)

    def body(weight_ref, core_ref, *refs):
        offset_refs, (ids_ref, low_ref, down_ref) = refs[:count], refs[count : count + 3]
        piece_refs = refs[count + 3 : 2 * count + 3]
        out_ref, *held = refs[len(refs) - count - 2 : -1]
        sems = refs[-1]
        own_ids = ids_ref[pl.ds(core_ref[0], 1), :]
        scale = jnp.zeros(own_ids.shape, F32)
        spread = []
        for a in range(adapters):
            scale = jnp.where(own_ids == a, weight_ref[a], scale)
            spread.append(jnp.where(own_ids == a, low_ref[...].astype(F32), 0.0))
        spread = jnp.concatenate(spread, axis=0).T.astype(BF16)
        scale = jnp.broadcast_to(scale, (rows, rows)).T[:, :1]
        copies = []
        for i, (piece, start) in enumerate(zip(pieces, starts)):
            own, chunk = slice(start, start + piece.shape[0]), piece.shape[1]
            at = pl.ds(pl.multiple_of(offset_refs[i][0], 128), chunk)
            term = dot_plain(spread[own], down_ref[:, at])
            total = piece_refs[i][...].astype(F32) + ADAPTER_SCALE * term
            held[i][...] = (scale[own] * total).astype(BF16)
            copies.append(pltpu.make_async_copy(held[i], out_ref.at[own, at], sems.at[i]))
            copies[-1].start()
        for copy in copies:
            copy.wait()

    args = [weight, core, *offsets, ids, low_out, down_t, *pieces]
    specs = {i: SMEM for i in range(2 + count)}
    aliases = None
    if into is not None:
        specs[len(args)] = ANY
        aliases = {len(args): 0}
        args.append(into)
    scratch = [pltpu.VMEM(p.shape, BF16) for p in pieces] + [pltpu.SemaphoreType.DMA((count,))]
    shape = array((rows, width), BF16)
    return call(body, shape, args, specs, out_specs=ANY, scratch=scratch, aliases=aliases)


def swap(value, axis, step):
    size = lax.axis_size(axis)
    return lax.ppermute(value, axis, [(i, i ^ step) for i in range(size)])


def pick(value, index):
    return lax.dynamic_index_in_dim(value, index, 0, keepdims=False)


def choose(values, index):
    out = values[0]
    for i in range(1, len(values)):
        out = jnp.where(index == i, values[i], out)
    return out


def after(value, *others):
    return lax.optimization_barrier((value, *others))[0]


def local(x, g, ids, owner_slot, w, down, up):
    rows = x.shape[0]
    adapters = owner_slot.shape[0]
    rank = up.shape[1]
    n, tensors, cores = lax.axis_size("dp"), lax.axis_size("tensor"), lax.axis_size("seq")
    z, t, c = lax.axis_index("dp"), lax.axis_index("tensor"), lax.axis_index("seq")
    core, place = one(c), one(z)
    slots = n * OWN_MAX
    labels = jnp.arange(adapters, dtype=jnp.int32)
    ids = ids.reshape(cores, rows)

    top = n // 2
    blocks = {0: g, top: swap(g, "dp", top)}

    def hand_on(froms, *ready):
        bit = top // 2
        while bit:
            for s in [s for s in blocks if s in froms]:
                blocks[s ^ bit] = swap(after(blocks[s], *ready), "dp", bit)
            bit //= 2

    hand_on(range(top))

    w_other = swap(w, "seq", 1)
    width = cores * w.shape[0]
    chunk = width // tensors
    first = None
    if tensors == cores:
        w_parts, first = [w, w_other], one(t ^ c)
    else:
        w_chip = jnp.where(c == 0, jnp.stack([w, w_other]), jnp.stack([w_other, w]))
        w_chip = w_chip.reshape(tensors, chunk, -1)
        w_parts = [pick(w_chip, t ^ k) for k in range(tensors)]

    parts, totals = {}, {}

    def product(s, *ready):
        made = multiply(after(blocks[s], *ready), w_parts, first)
        kept = made[0].astype(F32)
        for k in range(1, tensors):
            kept = kept + swap(made[k], "tensor", k).astype(F32)
        parts[s], totals[s] = made, kept.astype(BF16)

    down_t = down.transpose(1, 2, 0).reshape(adapters * rank, -1)
    up_t = up.reshape(adapters * rank, -1)
    low = project(core, after(ids, w_other), x, g, down_t, up_t, rank)
    lows = [low] + [swap(low, "tensor", s) for s in range(1, tensors)]

    product(0, low)
    card, low_out, mine, away = lift_down(owner_slot, core, ids, x, lows, slots)
    half = mine.shape[1]
    got = swap(after(away, blocks[top]), "seq", 1)
    *held, letter = chip_sums(place, card, mine, got, n)
    cards = {0: card}

    def post(bit, letter):
        known = list(cards)
        got = swap(letter, "dp", bit)
        for s in range(bit):
            total = held[s].astype(F32) + got[:, s * half : (s + 1) * half].astype(F32)
            held[s] = total.astype(BF16) if bit > 1 else total
        for i, s in enumerate(known):
            at = bit * half + i * rows
            cards[s ^ bit] = got[:, at : at + rows]

    post(top, letter)
    hand_on(range(top, n), low, *parts[0])
    order = [*range(top, n - 1), *range(1, top)]
    ready = [letter]
    for s in order:
        product(s, *ready)
        ready = parts[s]
    last = after(blocks[n - 1], *ready, totals[order[0]])
    away_parts = multiply(last, w_parts, first, range(1, tensors), CUTS)
    kept_parts = multiply(after(last, *away_parts), w_parts, first, (0,), CUTS)
    finals = []
    for j in range(CUTS):
        kept = after(kept_parts[j], *finals).astype(F32)
        for k in range(1, tensors):
            kept = kept + swap(away_parts[(k - 1) * CUTS + j], "tensor", k).astype(F32)
        finals.append(kept.astype(BF16))
    bit = top // 2
    while bit:
        letter = held[bit : 2 * bit] + [cards[s] for s in cards]
        post(bit, after(jnp.concatenate(letter, axis=1), finals[-1]))
        bit //= 2
    cards = [after(cards[s], finals[-1]) for s in range(n)]
    down_sum = after(held[0], finals[-1])
    all_ids = jnp.stack([v[rank : rank + cores] for v in cards]).astype(jnp.int32)
    counts = jnp.sum((all_ids.reshape(1, -1) == labels[:, None]).astype(F32), axis=1)
    weight = F32(n * cores * rows) / (F32(adapters) * counts)
    my_slots = z * OWN_MAX + jnp.arange(OWN_MAX, dtype=jnp.int32)
    slot_weight = ADAPTER_SCALE * jnp.sum(
        jnp.where(owner_slot[None, :] == my_slots[:, None], weight[None, :], 0.0), axis=1
    )
    down_grad = down_sum.reshape(OWN_MAX, rank, half) * slot_weight[:, None, None]
    down_grad = down_grad.transpose(2, 0, 1)

    back = [swap(totals[s], "dp", s) if s else totals[0] for s in range(n - 1)]
    last_back = [swap(v, "dp", n - 1) for v in finals]
    span = n // tensors
    low_bits, high_bits = z % span, z // span
    pieces, offsets, starts = [], [], []
    for r in range(span):
        for j in range(CUTS if r == span - 1 else 1):
            choices = [back[s] for s in range(r, n - 1, span)]
            start = j * (rows // CUTS)
            if r == span - 1:
                choices = [v[start : start + rows // CUTS] for v in choices] + [last_back[j]]
            choices[0] = after(choices[0], finals[-1], *(choices_before if j else ()))
            choices_before = choices
            for k in range(tensors):
                piece = choose(choices, t ^ k ^ high_bits)
                pieces.append(swap(piece, "tensor", k) if k else piece)
                offsets.append((r ^ low_bits) * width + (t ^ k) * chunk)
                starts.append(start)
    if chunk % 128 == 0:
        offsets = [one(v) for v in offsets]
        args = (weight, core, ids, low_out, down_t)
        late = len(pieces) - len(pieces)
        early = finish(*args, pieces[:late], offsets[:late], starts[:late]) if late else None
        input_gradient = finish(*args, pieces[late:], offsets[late:], starts[late:], into=early)
    else:
        base = jnp.zeros((rows, span * width), BF16)
        for piece, offset, start in zip(pieces, offsets, starts):
            base = lax.dynamic_update_slice(base, piece, (start, offset))
        own_match = (pick(ids, c)[:, None] == labels[None, :]).astype(F32)
        own_weight = jnp.sum(own_match * weight[None, :], axis=1)
        spread = (own_match.T.astype(BF16)[:, None, :] * low_out[None]).reshape(-1, rows)
        total = base.astype(F32) + ADAPTER_SCALE * dot_first(spread, down_t)
        input_gradient = (own_weight[:, None] * total).astype(BF16)

    up_mine, up_away = lift_up(
        owner_slot, core, place, cards, [blocks[s] for s in range(n)], rank
    )
    up_sum = up_mine + swap(up_away, "seq", 1)
    up_grad = up_sum.reshape(OWN_MAX, rank, -1) * slot_weight[:, None, None]
    return input_gradient, down_grad, up_grad


def solution(mesh):
    in_specs = (
        P(("groups", "dp", "seq"), "tensor"),
        P(("groups", "dp", "seq"), "tensor"),
        P(("groups", "dp")),
        P("groups"),
        P(("dp", "seq"), "tensor"),
        P(("groups", "tensor"), None, None),
        P("groups", None, "tensor"),
    )
    out_specs = (
        P(("groups", "dp", "seq"), "tensor"),
        P(("groups", "tensor", "seq"), "dp", None),
        P(("groups", "dp"), None, ("tensor", "seq")),
    )
    return jax.shard_map(local, mesh=mesh, in_specs=in_specs, out_specs=out_specs, check_vma=False)
```

```python
import jax
import jax.numpy as jnp
from jax import lax
from jax.experimental import pallas as pl
from jax.experimental.pallas import tpu as pltpu
from jax.sharding import PartitionSpec as P

OWN_MAX = 2
CUTS = 2
ADAPTER_SCALE = 2.0
F32 = jnp.float32
BF16 = jnp.bfloat16
VMEM = pl.BlockSpec(memory_space=pltpu.VMEM)
SMEM = pl.BlockSpec(memory_space=pltpu.SMEM)
ANY = pl.BlockSpec(memory_space=pl.ANY)


def dot_last(left, right):
    return lax.dot_general(left, right, (((1,), (1,)), ((), ())), preferred_element_type=F32)


def dot_plain(left, right):
    return lax.dot_general(left, right, (((1,), (0,)), ((), ())), preferred_element_type=F32)


def dot_first(left, right):
    return lax.dot_general(left, right, (((0,), (0,)), ((), ())), preferred_element_type=F32)


def call(body, out_shape, args, specs, out_specs=None, scratch=(), aliases=None):
    in_specs = [specs.get(i, VMEM) for i in range(len(args))]
    if out_specs is None:
        out_specs = jax.tree.map(lambda _: VMEM, out_shape)
    return pl.pallas_call(
        body,
        out_shape=out_shape,
        in_specs=in_specs,
        out_specs=out_specs,
        scratch_shapes=scratch,
        input_output_aliases=aliases or {},
        compiler_params=pltpu.CompilerParams(vmem_limit_bytes=12 << 20),
        cost_estimate=pl.CostEstimate(flops=1<<33, bytes_accessed=1<<25, transcendentals=0),
    )(*args)


def array(shape, dtype):
    return jax.ShapeDtypeStruct(shape, dtype)


def one(scalar):
    return scalar.reshape(1)


def multiply(piece, w_parts, first=None, chosen=None, cuts=1):
    parts = len(w_parts)
    chosen = range(parts) if chosen is None else chosen
    rows = piece.shape[0] // cuts

    def body(*refs):
        if first is None:
            refs = (None, *refs)
        piece_ref, ws, outs = refs[1], refs[2 : 2 + parts], refs[2 + parts :]

        def work(order):
            for i, k in enumerate(chosen):
                value = dot_last(piece_ref[...], ws[order[k]][...]).astype(BF16)
                for j in range(cuts):
                    outs[i * cuts + j][...] = value[j * rows : (j + 1) * rows]

        if first is None:
            work(range(parts))
        else:
            pl.when(refs[0][0] == 0)(lambda: work((0, 1)))
            pl.when(refs[0][0] == 1)(lambda: work((1, 0)))

    shapes = [array((rows, w_parts[k].shape[0]), BF16) for k in chosen for _ in range(cuts)]
    head = [] if first is None else [first]
    return list(call(body, shapes, [*head, piece, *w_parts], {i: SMEM for i in range(len(head))}))


def project(core, ids, x, g, down_t, up_t, rank):
    adapters = down_t.shape[0] // rank

    def body(core_ref, ids_ref, x_ref, g_ref, down_ref, up_ref, out_ref):
        own_ids = ids_ref[pl.ds(core_ref[0], 1), :]
        for i, (rows, factors) in enumerate(((x_ref, down_ref), (g_ref, up_ref))):
            every = dot_last(factors[...], rows[...])
            own = jnp.zeros((rank, every.shape[1]), F32)
            for a in range(adapters):
                own += jnp.where(own_ids == a, every[a * rank : (a + 1) * rank], 0.0)
            out_ref[i * rank : (i + 1) * rank] = own

    shape = array((2 * rank, x.shape[0]), F32)
    return call(body, shape, [core, ids, x, g, down_t, up_t], {0: SMEM})


def slot_row(ids, slot_ref, adapters):
    slot = jnp.zeros(ids.shape, jnp.int32)
    for a in range(adapters):
        slot = jnp.where(ids == a, slot_ref[a], slot)
    return slot


def lift_down(owner_slot, core, ids, x, lows, slots):
    adapters, cores = owner_slot.shape[0], ids.shape[0]
    rank = lows[0].shape[0] // 2
    rows, width = x.shape
    half = width // 2

    def body(slot_ref, core_ref, ids_ref, x_ref, *rest):
        low_refs = rest[: len(lows)]
        card_ref, low_ref, mine_ref, away_ref, spread_ref = rest[len(lows) :]
        low = low_refs[0][...]
        for ref in low_refs[1:]:
            low = low + ref[...]
        card_ref[...] = jnp.concatenate(
            [
                low[:rank],
                ids_ref[...].astype(F32),
                jnp.zeros((OWN_MAX * rank - rank - cores, rows), F32),
            ],
            axis=0,
        ).astype(BF16)
        low_out = low[rank:].astype(BF16)
        low_ref[...] = low_out
        core = core_ref[0]
        slot = slot_row(ids_ref[pl.ds(core, 1), :], slot_ref, adapters)
        for s in range(slots):
            part = jnp.where(slot == s, low_out.astype(F32), 0.0)
            spread_ref[s * rank : (s + 1) * rank] = part.astype(BF16)
        for ref, part in ((mine_ref, core), (away_ref, 1 - core)):
            at = pl.ds(pl.multiple_of(part * half, 128), half)
            ref[...] = dot_plain(spread_ref[...], x_ref[:, at]).astype(BF16)

    wide = array((slots * rank, half), BF16)
    shapes = [array((OWN_MAX * rank, rows), BF16), array((rank, rows), BF16), wide, wide]
    scratch = [pltpu.VMEM((slots * rank, rows), BF16)]
    args = [owner_slot, core, ids, x, *lows]
    return call(body, shapes, args, {0: SMEM, 1: SMEM}, scratch=scratch)


def chip_sums(place, card, mine, got, n):
    deep, half, rows = mine.shape[0] // n, mine.shape[1], card.shape[1]
    top = n // 2

    def body(place_ref, card_ref, mine_ref, got_ref, *outs):
        for s in range(n):
            at = pl.ds(pl.multiple_of((place_ref[0] ^ s) * deep, 16), deep)
            total = (mine_ref[at].astype(F32) + got_ref[at].astype(F32)).astype(BF16)
            if s < top:
                outs[s][...] = total
            else:
                outs[top][:, (s - top) * half : (s - top + 1) * half] = total
        outs[top][:, top * half :] = card_ref[...]

    shapes = [array((deep, half), BF16)] * top + [array((deep, top * half + rows), BF16)]
    return list(call(body, shapes, [place, card, mine, got], {0: SMEM}))


def lift_up(owner_slot, core, place, cards, blocks, rank):
    n, adapters = len(blocks), owner_slot.shape[0]
    width = blocks[0].shape[1]
    half = width // 2

    def body(slot_ref, core_ref, place_ref, *refs):
        card_refs, block_refs, outs = refs[:n], refs[n : 2 * n], refs[2 * n :]
        core, first = core_ref[0], place_ref[0] * OWN_MAX
        lifts = []
        for ref in card_refs:
            card = ref[...].astype(F32)
            ids = jnp.where(core == 0, card[rank : rank + 1], card[rank + 1 : rank + 2])
            slot = slot_row(ids.astype(jnp.int32), slot_ref, adapters)
            lift = [jnp.where(slot == first + o, card[:rank], 0.0) for o in range(OWN_MAX)]
            lifts.append(jnp.concatenate(lift, axis=0).astype(BF16))
        if half % 128:
            outs[0][...] = sum(dot_plain(a, b[...]) for a, b in zip(lifts, block_refs))
            return
        for ref, part in zip(outs, (core, 1 - core)):
            at = pl.ds(pl.multiple_of(part * half, 128), half)
            ref[...] = sum(dot_plain(a, b[:, at]) for a, b in zip(lifts, block_refs))

    deep = OWN_MAX * rank
    shapes = [array((deep, width), F32)] if half % 128 else [array((deep, half), F32)] * 2
    args = [owner_slot, core, place, *cards, *blocks]
    out = call(body, shapes, args, {0: SMEM, 1: SMEM, 2: SMEM})
    if half % 128:
        at = core[0] * half
        return [lax.dynamic_slice_in_dim(out[0], p, half, 1) for p in (at, half - at)]
    return out


def adapter_rows(core, ids, low_out, down_t):
    rows, width = ids.shape[1], down_t.shape[1]
    adapters = down_t.shape[0] // low_out.shape[0]

    def body(core_ref, ids_ref, low_ref, down_ref, out_ref):
        own_ids = ids_ref[pl.ds(core_ref[0], 1), :]
        low = low_ref[...].astype(F32)
        spread = [jnp.where(own_ids == a, low, 0.0) for a in range(adapters)]
        spread = jnp.concatenate(spread, axis=0).T.astype(BF16)
        out_ref[...] = ADAPTER_SCALE * dot_plain(spread, down_ref[...])

    return call(body, array((rows, width), F32), [core, ids, low_out, down_t], {0: SMEM})


def row_scales(weight, core, ids):
    rows = ids.shape[1]

    def body(weight_ref, core_ref, ids_ref, out_ref):
        own_ids = ids_ref[pl.ds(core_ref[0], 1), :]
        scale = jnp.zeros(own_ids.shape, F32)
        for a in range(weight.shape[0]):
            scale = jnp.where(own_ids == a, weight_ref[a], scale)
        out_ref[...] = jnp.broadcast_to(scale, (rows, rows)).T

    return call(body, array((rows, rows), F32), [weight, core, ids], {0: SMEM, 1: SMEM})


def finish(scale, term, pieces, offsets, starts, into=None):
    count = len(pieces)

    def body(*refs):
        offset_refs, (scale_ref, term_ref) = refs[:count], refs[count : count + 2]
        piece_refs = refs[count + 2 : 2 * count + 2]
        out_ref, *held = refs[len(refs) - count - 2 : -1]
        sems = refs[-1]
        copies = []
        for i, (piece, start) in enumerate(zip(pieces, starts)):
            own, chunk = slice(start, start + piece.shape[0]), piece.shape[1]
            at = pl.ds(pl.multiple_of(offset_refs[i][0], 128), chunk)
            total = piece_refs[i][...].astype(F32) + term_ref[own, at]
            held[i][...] = (scale_ref[own, :1] * total).astype(BF16)
            copies.append(pltpu.make_async_copy(held[i], out_ref.at[own, at], sems.at[i]))
            copies[-1].start()
        for copy in copies:
            copy.wait()

    args = [*offsets, scale, term, *pieces]
    specs = {i: SMEM for i in range(count)}
    aliases = None
    if into is not None:
        specs[len(args)] = ANY
        aliases = {len(args): 0}
        args.append(into)
    scratch = [pltpu.VMEM(p.shape, BF16) for p in pieces] + [pltpu.SemaphoreType.DMA((count,))]
    shape = array(term.shape, BF16)
    return call(body, shape, args, specs, out_specs=ANY, scratch=scratch, aliases=aliases)


def swap(value, axis, step):
    size = lax.axis_size(axis)
    return lax.ppermute(value, axis, [(i, i ^ step) for i in range(size)])


def pick(value, index):
    return lax.dynamic_index_in_dim(value, index, 0, keepdims=False)


def choose(values, index):
    out = values[0]
    for i in range(1, len(values)):
        out = jnp.where(index == i, values[i], out)
    return out


def after(value, *others):
    return lax.optimization_barrier((value, *others))[0]


def local(x, g, ids, owner_slot, w, down, up):
    rows = x.shape[0]
    adapters = owner_slot.shape[0]
    rank = up.shape[1]
    n, tensors, cores = lax.axis_size("dp"), lax.axis_size("tensor"), lax.axis_size("seq")
    z, t, c = lax.axis_index("dp"), lax.axis_index("tensor"), lax.axis_index("seq")
    core, place = one(c), one(z)
    slots = n * OWN_MAX
    labels = jnp.arange(adapters, dtype=jnp.int32)
    ids = ids.reshape(cores, rows)

    top = n // 2
    blocks = {0: g, top: swap(g, "dp", top)}

    def hand_on(froms, *ready):
        bit = top // 2
        while bit:
            for s in [s for s in blocks if s in froms]:
                blocks[s ^ bit] = swap(after(blocks[s], *ready), "dp", bit)
            bit //= 2

    hand_on(range(top))

    w_other = swap(w, "seq", 1)
    width = cores * w.shape[0]
    chunk = width // tensors
    first = None
    if tensors == cores:
        w_parts, first = [w, w_other], one(t ^ c)
    else:
        w_chip = jnp.where(c == 0, jnp.stack([w, w_other]), jnp.stack([w_other, w]))
        w_chip = w_chip.reshape(tensors, chunk, -1)
        w_parts = [pick(w_chip, t ^ k) for k in range(tensors)]

    parts, totals = {}, {}

    def product(s, *ready):
        made = multiply(after(blocks[s], *ready), w_parts, first)
        kept = made[0].astype(F32)
        for k in range(1, tensors):
            kept = kept + swap(made[k], "tensor", k).astype(F32)
        parts[s], totals[s] = made, kept.astype(BF16)

    down_t = down.transpose(1, 2, 0).reshape(adapters * rank, -1)
    up_t = up.reshape(adapters * rank, -1)
    low = project(core, after(ids, w_other), x, g, down_t, up_t, rank)
    lows = [low] + [swap(low, "tensor", s) for s in range(1, tensors)]

    product(0, low)
    card, low_out, mine, away = lift_down(owner_slot, core, ids, x, lows, slots)
    half = mine.shape[1]
    got = swap(after(away, blocks[top]), "seq", 1)
    *held, letter = chip_sums(place, card, mine, got, n)
    cards = {0: card}

    def post(bit, letter):
        known = list(cards)
        got = swap(letter, "dp", bit)
        for s in range(bit):
            total = held[s].astype(F32) + got[:, s * half : (s + 1) * half].astype(F32)
            held[s] = total.astype(BF16) if bit > 1 else total
        for i, s in enumerate(known):
            at = bit * half + i * rows
            cards[s ^ bit] = got[:, at : at + rows]

    post(top, letter)
    term = adapter_rows(core, ids, low_out, down_t)
    hand_on(range(top, n), low, *parts[0])
    order = [*range(top, n - 1), *range(1, top)]
    ready = [letter]
    for s in order:
        product(s, *ready)
        ready = parts[s]
    last = after(blocks[n - 1], *ready, totals[order[0]])
    away_parts = multiply(last, w_parts, first, range(1, tensors), CUTS)
    kept_parts = multiply(after(last, *away_parts), w_parts, first, (0,), CUTS)
    finals = []
    for j in range(CUTS):
        kept = after(kept_parts[j], *finals).astype(F32)
        for k in range(1, tensors):
            kept = kept + swap(away_parts[(k - 1) * CUTS + j], "tensor", k).astype(F32)
        finals.append(kept.astype(BF16))
    bit = top // 2
    while bit:
        letter = held[bit : 2 * bit] + [cards[s] for s in cards]
        post(bit, after(jnp.concatenate(letter, axis=1), finals[-1]))
        bit //= 2
    cards = [after(cards[s], finals[-1]) for s in range(n)]
    down_sum = after(held[0], finals[-1])
    all_ids = jnp.stack([v[rank : rank + cores] for v in cards]).astype(jnp.int32)
    counts = jnp.sum((all_ids.reshape(1, -1) == labels[:, None]).astype(F32), axis=1)
    weight = F32(n * cores * rows) / (F32(adapters) * counts)
    my_slots = z * OWN_MAX + jnp.arange(OWN_MAX, dtype=jnp.int32)
    slot_weight = ADAPTER_SCALE * jnp.sum(
        jnp.where(owner_slot[None, :] == my_slots[:, None], weight[None, :], 0.0), axis=1
    )
    down_grad = down_sum.reshape(OWN_MAX, rank, half) * slot_weight[:, None, None]
    down_grad = down_grad.transpose(2, 0, 1)

    back = [swap(totals[s], "dp", s) if s else totals[0] for s in range(n - 1)]
    last_back = [swap(v, "dp", n - 1) for v in finals]
    span = n // tensors
    low_bits, high_bits = z % span, z // span
    pieces, offsets, starts = [], [], []
    for r in range(span):
        for j in range(CUTS if r == span - 1 else 1):
            choices = [back[s] for s in range(r, n - 1, span)]
            start = j * (rows // CUTS)
            if r == span - 1:
                choices = [v[start : start + rows // CUTS] for v in choices] + [last_back[j]]
            choices[0] = after(choices[0], finals[-1], *(choices_before if j else ()))
            choices_before = choices
            for k in range(tensors):
                piece = choose(choices, t ^ k ^ high_bits)
                pieces.append(swap(piece, "tensor", k) if k else piece)
                offsets.append((r ^ low_bits) * width + (t ^ k) * chunk)
                starts.append(start)
    if chunk % 128 == 0:
        offsets = [one(v) for v in offsets]
        args = (row_scales(weight, core, ids), term)
        late = len(pieces) - len(pieces)
        early = finish(*args, pieces[:late], offsets[:late], starts[:late]) if late else None
        input_gradient = finish(*args, pieces[late:], offsets[late:], starts[late:], into=early)
    else:
        base = jnp.zeros((rows, span * width), BF16)
        for piece, offset, start in zip(pieces, offsets, starts):
            base = lax.dynamic_update_slice(base, piece, (start, offset))
        own_match = (pick(ids, c)[:, None] == labels[None, :]).astype(F32)
        own_weight = jnp.sum(own_match * weight[None, :], axis=1)
        input_gradient = (own_weight[:, None] * (base.astype(F32) + term)).astype(BF16)

    up_mine, up_away = lift_up(
        owner_slot, core, place, cards, [blocks[s] for s in range(n)], rank
    )
    up_sum = up_mine + swap(up_away, "seq", 1)
    up_grad = up_sum.reshape(OWN_MAX, rank, -1) * slot_weight[:, None, None]
    return input_gradient, down_grad, up_grad


def solution(mesh):
    in_specs = (
        P(("groups", "dp", "seq"), "tensor"),
        P(("groups", "dp", "seq"), "tensor"),
        P(("groups", "dp")),
        P("groups"),
        P(("dp", "seq"), "tensor"),
        P(("groups", "tensor"), None, None),
        P("groups", None, "tensor"),
    )
    out_specs = (
        P(("groups", "dp", "seq"), "tensor"),
        P(("groups", "tensor", "seq"), "dp", None),
        P(("groups", "dp"), None, ("tensor", "seq")),
    )
    return jax.shard_map(local, mesh=mesh, in_specs=in_specs, out_specs=out_specs, check_vma=False)
```

```python
import jax
import jax.numpy as jnp
from jax import lax
from jax.experimental import pallas as pl
from jax.experimental.pallas import tpu as pltpu
from jax.sharding import PartitionSpec as P

OWN_MAX = 2
CUTS = 2
ADAPTER_SCALE = 2.0
F32 = jnp.float32
BF16 = jnp.bfloat16
VMEM = pl.BlockSpec(memory_space=pltpu.VMEM)
SMEM = pl.BlockSpec(memory_space=pltpu.SMEM)
ANY = pl.BlockSpec(memory_space=pl.ANY)


def dot_last(left, right):
    return lax.dot_general(left, right, (((1,), (1,)), ((), ())), preferred_element_type=F32)


def dot_plain(left, right):
    return lax.dot_general(left, right, (((1,), (0,)), ((), ())), preferred_element_type=F32)


def dot_first(left, right):
    return lax.dot_general(left, right, (((0,), (0,)), ((), ())), preferred_element_type=F32)


def call(body, out_shape, args, specs, out_specs=None, scratch=(), aliases=None):
    in_specs = [specs.get(i, VMEM) for i in range(len(args))]
    if out_specs is None:
        out_specs = jax.tree.map(lambda _: VMEM, out_shape)
    return pl.pallas_call(
        body,
        out_shape=out_shape,
        in_specs=in_specs,
        out_specs=out_specs,
        scratch_shapes=scratch,
        input_output_aliases=aliases or {},
        compiler_params=pltpu.CompilerParams(vmem_limit_bytes=12 << 20),
        cost_estimate=pl.CostEstimate(flops=1<<33, bytes_accessed=1<<25, transcendentals=0),
    )(*args)


def array(shape, dtype):
    return jax.ShapeDtypeStruct(shape, dtype)


def one(scalar):
    return scalar.reshape(1)


def multiply(piece, w_parts, first=None, chosen=None, cuts=1):
    parts = len(w_parts)
    chosen = range(parts) if chosen is None else chosen
    rows = piece.shape[0] // cuts

    def body(*refs):
        if first is None:
            refs = (None, *refs)
        piece_ref, ws, outs = refs[1], refs[2 : 2 + parts], refs[2 + parts :]

        def work(order):
            for i, k in enumerate(chosen):
                value = dot_last(piece_ref[...], ws[order[k]][...]).astype(BF16)
                for j in range(cuts):
                    outs[i * cuts + j][...] = value[j * rows : (j + 1) * rows]

        if first is None:
            work(range(parts))
        else:
            pl.when(refs[0][0] == 0)(lambda: work((0, 1)))
            pl.when(refs[0][0] == 1)(lambda: work((1, 0)))

    shapes = [array((rows, w_parts[k].shape[0]), BF16) for k in chosen for _ in range(cuts)]
    head = [] if first is None else [first]
    return list(call(body, shapes, [*head, piece, *w_parts], {i: SMEM for i in range(len(head))}))


def project(core, ids, x, g, down_t, up_t, rank):
    adapters = down_t.shape[0] // rank

    def body(core_ref, ids_ref, x_ref, g_ref, down_ref, up_ref, out_ref):
        own_ids = ids_ref[pl.ds(core_ref[0], 1), :]
        for i, (rows, factors) in enumerate(((x_ref, down_ref), (g_ref, up_ref))):
            every = dot_last(factors[...], rows[...])
            own = jnp.zeros((rank, every.shape[1]), F32)
            for a in range(adapters):
                own += jnp.where(own_ids == a, every[a * rank : (a + 1) * rank], 0.0)
            out_ref[i * rank : (i + 1) * rank] = own

    shape = array((2 * rank, x.shape[0]), F32)
    return call(body, shape, [core, ids, x, g, down_t, up_t], {0: SMEM})


def slot_row(ids, slot_ref, adapters):
    slot = jnp.zeros(ids.shape, jnp.int32)
    for a in range(adapters):
        slot = jnp.where(ids == a, slot_ref[a], slot)
    return slot


def lift_down(owner_slot, core, ids, x, lows, slots):
    adapters, cores = owner_slot.shape[0], ids.shape[0]
    rank = lows[0].shape[0] // 2
    rows, width = x.shape
    half = width // 2

    def body(slot_ref, core_ref, ids_ref, x_ref, *rest):
        low_refs = rest[: len(lows)]
        card_ref, low_ref, mine_ref, away_ref, spread_ref = rest[len(lows) :]
        low = low_refs[0][...]
        for ref in low_refs[1:]:
            low = low + ref[...]
        card_ref[...] = jnp.concatenate(
            [
                low[:rank],
                ids_ref[...].astype(F32),
                jnp.zeros((OWN_MAX * rank - rank - cores, rows), F32),
            ],
            axis=0,
        ).astype(BF16)
        low_out = low[rank:].astype(BF16)
        low_ref[...] = low_out
        core = core_ref[0]
        slot = slot_row(ids_ref[pl.ds(core, 1), :], slot_ref, adapters)
        for s in range(slots):
            part = jnp.where(slot == s, low_out.astype(F32), 0.0)
            spread_ref[s * rank : (s + 1) * rank] = part.astype(BF16)
        for ref, part in ((mine_ref, core), (away_ref, 1 - core)):
            at = pl.ds(pl.multiple_of(part * half, 128), half)
            ref[...] = dot_plain(spread_ref[...], x_ref[:, at]).astype(BF16)

    wide = array((slots * rank, half), BF16)
    shapes = [array((OWN_MAX * rank, rows), BF16), array((rank, rows), BF16), wide, wide]
    scratch = [pltpu.VMEM((slots * rank, rows), BF16)]
    args = [owner_slot, core, ids, x, *lows]
    return call(body, shapes, args, {0: SMEM, 1: SMEM}, scratch=scratch)


def chip_sums(place, card, mine, got, n):
    deep, half, rows = mine.shape[0] // n, mine.shape[1], card.shape[1]
    top = n // 2

    def body(place_ref, card_ref, mine_ref, got_ref, *outs):
        for s in range(n):
            at = pl.ds(pl.multiple_of((place_ref[0] ^ s) * deep, 16), deep)
            total = (mine_ref[at].astype(F32) + got_ref[at].astype(F32)).astype(BF16)
            if s < top:
                outs[s][...] = total
            else:
                outs[top][:, (s - top) * half : (s - top + 1) * half] = total
        outs[top][:, top * half :] = card_ref[...]

    shapes = [array((deep, half), BF16)] * top + [array((deep, top * half + rows), BF16)]
    return list(call(body, shapes, [place, card, mine, got], {0: SMEM}))


def lift_up(owner_slot, core, place, cards, blocks, rank):
    n, adapters = len(blocks), owner_slot.shape[0]
    width = blocks[0].shape[1]
    half = width // 2

    def body(slot_ref, core_ref, place_ref, *refs):
        card_refs, block_refs, outs = refs[:n], refs[n : 2 * n], refs[2 * n :]
        core, first = core_ref[0], place_ref[0] * OWN_MAX
        lifts = []
        for ref in card_refs:
            card = ref[...].astype(F32)
            ids = jnp.where(core == 0, card[rank : rank + 1], card[rank + 1 : rank + 2])
            slot = slot_row(ids.astype(jnp.int32), slot_ref, adapters)
            lift = [jnp.where(slot == first + o, card[:rank], 0.0) for o in range(OWN_MAX)]
            lifts.append(jnp.concatenate(lift, axis=0).astype(BF16))
        if half % 128:
            outs[0][...] = sum(dot_plain(a, b[...]) for a, b in zip(lifts, block_refs))
            return
        for ref, part in zip(outs, (core, 1 - core)):
            at = pl.ds(pl.multiple_of(part * half, 128), half)
            ref[...] = sum(dot_plain(a, b[:, at]) for a, b in zip(lifts, block_refs))

    deep = OWN_MAX * rank
    shapes = [array((deep, width), F32)] if half % 128 else [array((deep, half), F32)] * 2
    args = [owner_slot, core, place, *cards, *blocks]
    out = call(body, shapes, args, {0: SMEM, 1: SMEM, 2: SMEM})
    if half % 128:
        at = core[0] * half
        return [lax.dynamic_slice_in_dim(out[0], p, half, 1) for p in (at, half - at)]
    return out


def adapter_rows(core, ids, low_out, down_t):
    rows, width = ids.shape[1], down_t.shape[1]
    adapters = down_t.shape[0] // low_out.shape[0]

    def body(core_ref, ids_ref, low_ref, down_ref, out_ref):
        own_ids = ids_ref[pl.ds(core_ref[0], 1), :]
        low = low_ref[...].astype(F32)
        spread = [jnp.where(own_ids == a, low, 0.0) for a in range(adapters)]
        spread = jnp.concatenate(spread, axis=0).T.astype(BF16)
        out_ref[...] = ADAPTER_SCALE * dot_plain(spread, down_ref[...])

    return call(body, array((rows, width), F32), [core, ids, low_out, down_t], {0: SMEM})


def row_scales(weight, core, ids):
    rows = ids.shape[1]

    def body(weight_ref, core_ref, ids_ref, out_ref):
        own_ids = ids_ref[pl.ds(core_ref[0], 1), :]
        scale = jnp.zeros(own_ids.shape, F32)
        for a in range(weight.shape[0]):
            scale = jnp.where(own_ids == a, weight_ref[a], scale)
        out_ref[...] = jnp.broadcast_to(scale, (rows, rows)).T

    return call(body, array((rows, rows), F32), [weight, core, ids], {0: SMEM, 1: SMEM})


def finish(scale, term, pieces, offsets, starts, into=None):
    count = len(pieces)

    def body(*refs):
        offset_refs, (scale_ref, term_ref) = refs[:count], refs[count : count + 2]
        piece_refs = refs[count + 2 : 2 * count + 2]
        out_ref, *held = refs[len(refs) - count - 2 : -1]
        sems = refs[-1]
        copies = []
        for i, (piece, start) in enumerate(zip(pieces, starts)):
            own, chunk = slice(start, start + piece.shape[0]), piece.shape[1]
            at = pl.ds(pl.multiple_of(offset_refs[i][0], 128), chunk)
            total = piece_refs[i][...].astype(F32) + term_ref[own, at]
            held[i][...] = (scale_ref[own, :1] * total).astype(BF16)
            copies.append(pltpu.make_async_copy(held[i], out_ref.at[own, at], sems.at[i]))
            copies[-1].start()
        for copy in copies:
            copy.wait()

    args = [*offsets, scale, term, *pieces]
    specs = {i: SMEM for i in range(count)}
    aliases = None
    if into is not None:
        specs[len(args)] = ANY
        aliases = {len(args): 0}
        args.append(into)
    scratch = [pltpu.VMEM(p.shape, BF16) for p in pieces] + [pltpu.SemaphoreType.DMA((count,))]
    shape = array(term.shape, BF16)
    return call(body, shape, args, specs, out_specs=ANY, scratch=scratch, aliases=aliases)


def swap(value, axis, step):
    size = lax.axis_size(axis)
    return lax.ppermute(value, axis, [(i, i ^ step) for i in range(size)])


def pick(value, index):
    return lax.dynamic_index_in_dim(value, index, 0, keepdims=False)


def choose(values, index):
    out = values[0]
    for i in range(1, len(values)):
        out = jnp.where(index == i, values[i], out)
    return out


def after(value, *others):
    return lax.optimization_barrier((value, *others))[0]


def local(x, g, ids, owner_slot, w, down, up):
    rows = x.shape[0]
    adapters = owner_slot.shape[0]
    rank = up.shape[1]
    n, tensors, cores = lax.axis_size("dp"), lax.axis_size("tensor"), lax.axis_size("seq")
    z, t, c = lax.axis_index("dp"), lax.axis_index("tensor"), lax.axis_index("seq")
    core, place = one(c), one(z)
    slots = n * OWN_MAX
    labels = jnp.arange(adapters, dtype=jnp.int32)
    ids = ids.reshape(cores, rows)

    top = n // 2
    blocks = {0: g, top: swap(g, "dp", top)}

    def hand_on(froms, *ready):
        bit = top // 2
        while bit:
            for s in [s for s in blocks if s in froms]:
                blocks[s ^ bit] = swap(after(blocks[s], *ready), "dp", bit)
            bit //= 2

    hand_on(range(top))

    w_other = swap(w, "seq", 1)
    width = cores * w.shape[0]
    chunk = width // tensors
    first = None
    if tensors == cores:
        w_parts, first = [w, w_other], one(t ^ c)
    else:
        w_chip = jnp.where(c == 0, jnp.stack([w, w_other]), jnp.stack([w_other, w]))
        w_chip = w_chip.reshape(tensors, chunk, -1)
        w_parts = [pick(w_chip, t ^ k) for k in range(tensors)]

    parts, totals = {}, {}

    def product(s, *ready):
        made = multiply(after(blocks[s], *ready), w_parts, first)
        kept = made[0].astype(F32)
        for k in range(1, tensors):
            kept = kept + swap(made[k], "tensor", k).astype(F32)
        parts[s], totals[s] = made, kept.astype(BF16)

    down_t = down.transpose(1, 2, 0).reshape(adapters * rank, -1)
    up_t = up.reshape(adapters * rank, -1)
    low = project(core, after(ids, w_other), x, g, down_t, up_t, rank)
    lows = [low] + [swap(low, "tensor", s) for s in range(1, tensors)]

    product(0, low)
    card, low_out, mine, away = lift_down(owner_slot, core, ids, x, lows, slots)
    half = mine.shape[1]
    got = swap(after(away, blocks[top]), "seq", 1)
    *held, letter = chip_sums(place, card, mine, got, n)
    cards = {0: card}

    def post(bit, letter):
        known = list(cards)
        got = swap(letter, "dp", bit)
        for s in range(bit):
            total = held[s].astype(F32) + got[:, s * half : (s + 1) * half].astype(F32)
            held[s] = total.astype(BF16) if bit > 1 else total
        for i, s in enumerate(known):
            at = bit * half + i * rows
            cards[s ^ bit] = got[:, at : at + rows]

    post(top, letter)
    term = adapter_rows(core, ids, low_out, down_t)
    hand_on(range(top, n), card, *parts[0])
    order = [*range(top, n - 1), *range(1, top)]
    ready = [letter]
    for s in order:
        product(s, *ready)
        ready = parts[s]
    last = after(blocks[n - 1], *ready, totals[order[0]])
    away_parts = multiply(last, w_parts, first, range(1, tensors), CUTS)
    kept_parts = multiply(after(last, *away_parts), w_parts, first, (0,), CUTS)
    finals = []
    for j in range(CUTS):
        kept = after(kept_parts[j], *finals).astype(F32)
        for k in range(1, tensors):
            kept = kept + swap(away_parts[(k - 1) * CUTS + j], "tensor", k).astype(F32)
        finals.append(kept.astype(BF16))
    bit = top // 2
    while bit:
        letter = held[bit : 2 * bit] + [cards[s] for s in cards]
        post(bit, after(jnp.concatenate(letter, axis=1), finals[-1]))
        bit //= 2
    cards = [after(cards[s], finals[-1]) for s in range(n)]
    down_sum = after(held[0], finals[-1])
    all_ids = jnp.stack([v[rank : rank + cores] for v in cards]).astype(jnp.int32)
    counts = jnp.sum((all_ids.reshape(1, -1) == labels[:, None]).astype(F32), axis=1)
    weight = F32(n * cores * rows) / (F32(adapters) * counts)
    my_slots = z * OWN_MAX + jnp.arange(OWN_MAX, dtype=jnp.int32)
    slot_weight = ADAPTER_SCALE * jnp.sum(
        jnp.where(owner_slot[None, :] == my_slots[:, None], weight[None, :], 0.0), axis=1
    )
    down_grad = down_sum.reshape(OWN_MAX, rank, half) * slot_weight[:, None, None]
    down_grad = down_grad.transpose(2, 0, 1)

    back = [swap(totals[s], "dp", s) if s else totals[0] for s in range(n - 1)]
    last_back = [swap(v, "dp", n - 1) for v in finals]
    span = n // tensors
    low_bits, high_bits = z % span, z // span
    pieces, offsets, starts = [], [], []
    for r in range(span):
        for j in range(CUTS if r == span - 1 else 1):
            choices = [back[s] for s in range(r, n - 1, span)]
            start = j * (rows // CUTS)
            if r == span - 1:
                choices = [v[start : start + rows // CUTS] for v in choices] + [last_back[j]]
            choices[0] = after(choices[0], finals[-1], *(choices_before if j else ()))
            choices_before = choices
            for k in range(tensors):
                piece = choose(choices, t ^ k ^ high_bits)
                pieces.append(swap(piece, "tensor", k) if k else piece)
                offsets.append((r ^ low_bits) * width + (t ^ k) * chunk)
                starts.append(start)
    if chunk % 128 == 0:
        offsets = [one(v) for v in offsets]
        args = (row_scales(weight, core, ids), term)
        late = len(pieces) - len(pieces)
        early = finish(*args, pieces[:late], offsets[:late], starts[:late]) if late else None
        input_gradient = finish(*args, pieces[late:], offsets[late:], starts[late:], into=early)
    else:
        base = jnp.zeros((rows, span * width), BF16)
        for piece, offset, start in zip(pieces, offsets, starts):
            base = lax.dynamic_update_slice(base, piece, (start, offset))
        own_match = (pick(ids, c)[:, None] == labels[None, :]).astype(F32)
        own_weight = jnp.sum(own_match * weight[None, :], axis=1)
        input_gradient = (own_weight[:, None] * (base.astype(F32) + term)).astype(BF16)

    up_mine, up_away = lift_up(
        owner_slot, core, place, cards, [blocks[s] for s in range(n)], rank
    )
    up_sum = up_mine + swap(up_away, "seq", 1)
    up_grad = up_sum.reshape(OWN_MAX, rank, -1) * slot_weight[:, None, None]
    return input_gradient, down_grad, up_grad


def solution(mesh):
    in_specs = (
        P(("groups", "dp", "seq"), "tensor"),
        P(("groups", "dp", "seq"), "tensor"),
        P(("groups", "dp")),
        P("groups"),
        P(("dp", "seq"), "tensor"),
        P(("groups", "tensor"), None, None),
        P("groups", None, "tensor"),
    )
    out_specs = (
        P(("groups", "dp", "seq"), "tensor"),
        P(("groups", "tensor", "seq"), "dp", None),
        P(("groups", "dp"), None, ("tensor", "seq")),
    )
    return jax.shard_map(local, mesh=mesh, in_specs=in_specs, out_specs=out_specs, check_vma=False)
```

```python
import jax
import jax.numpy as jnp
from jax import lax
from jax.experimental import pallas as pl
from jax.experimental.pallas import tpu as pltpu
from jax.sharding import PartitionSpec as P

OWN_MAX = 2
CUTS = 2
ADAPTER_SCALE = 2.0
F32 = jnp.float32
BF16 = jnp.bfloat16
VMEM = pl.BlockSpec(memory_space=pltpu.VMEM)
SMEM = pl.BlockSpec(memory_space=pltpu.SMEM)
ANY = pl.BlockSpec(memory_space=pl.ANY)


def dot_last(left, right):
    return lax.dot_general(left, right, (((1,), (1,)), ((), ())), preferred_element_type=F32)


def dot_plain(left, right):
    return lax.dot_general(left, right, (((1,), (0,)), ((), ())), preferred_element_type=F32)


def dot_first(left, right):
    return lax.dot_general(left, right, (((0,), (0,)), ((), ())), preferred_element_type=F32)


def call(body, out_shape, args, specs, out_specs=None, scratch=(), aliases=None):
    in_specs = [specs.get(i, VMEM) for i in range(len(args))]
    if out_specs is None:
        out_specs = jax.tree.map(lambda _: VMEM, out_shape)
    return pl.pallas_call(
        body,
        out_shape=out_shape,
        in_specs=in_specs,
        out_specs=out_specs,
        scratch_shapes=scratch,
        input_output_aliases=aliases or {},
        compiler_params=pltpu.CompilerParams(vmem_limit_bytes=12 << 20),
        cost_estimate=pl.CostEstimate(flops=1<<33, bytes_accessed=1<<25, transcendentals=0),
    )(*args)


def array(shape, dtype):
    return jax.ShapeDtypeStruct(shape, dtype)


def one(scalar):
    return scalar.reshape(1)


def multiply(piece, w_parts, first=None, chosen=None, cuts=1):
    parts = len(w_parts)
    chosen = range(parts) if chosen is None else chosen
    rows = piece.shape[0] // cuts

    def body(*refs):
        if first is None:
            refs = (None, *refs)
        piece_ref, ws, outs = refs[1], refs[2 : 2 + parts], refs[2 + parts :]

        def work(order):
            for i, k in enumerate(chosen):
                value = dot_last(piece_ref[...], ws[order[k]][...]).astype(BF16)
                for j in range(cuts):
                    outs[i * cuts + j][...] = value[j * rows : (j + 1) * rows]

        if first is None:
            work(range(parts))
        else:
            pl.when(refs[0][0] == 0)(lambda: work((0, 1)))
            pl.when(refs[0][0] == 1)(lambda: work((1, 0)))

    shapes = [array((rows, w_parts[k].shape[0]), BF16) for k in chosen for _ in range(cuts)]
    head = [] if first is None else [first]
    return list(call(body, shapes, [*head, piece, *w_parts], {i: SMEM for i in range(len(head))}))


def project(core, ids, x, g, down_t, up_t, rank):
    adapters = down_t.shape[0] // rank

    def body(core_ref, ids_ref, x_ref, g_ref, down_ref, up_ref, out_ref):
        own_ids = ids_ref[pl.ds(core_ref[0], 1), :]
        for i, (rows, factors) in enumerate(((x_ref, down_ref), (g_ref, up_ref))):
            every = dot_last(factors[...], rows[...])
            own = jnp.zeros((rank, every.shape[1]), F32)
            for a in range(adapters):
                own += jnp.where(own_ids == a, every[a * rank : (a + 1) * rank], 0.0)
            out_ref[i * rank : (i + 1) * rank] = own

    shape = array((2 * rank, x.shape[0]), F32)
    return call(body, shape, [core, ids, x, g, down_t, up_t], {0: SMEM})


def slot_row(ids, slot_ref, adapters):
    slot = jnp.zeros(ids.shape, jnp.int32)
    for a in range(adapters):
        slot = jnp.where(ids == a, slot_ref[a], slot)
    return slot


def lift_down(owner_slot, core, ids, x, lows, slots):
    adapters, cores = owner_slot.shape[0], ids.shape[0]
    rank = lows[0].shape[0] // 2
    rows, width = x.shape
    half = width // 2

    def body(slot_ref, core_ref, ids_ref, x_ref, *rest):
        low_refs = rest[: len(lows)]
        card_ref, low_ref, mine_ref, away_ref, spread_ref = rest[len(lows) :]
        low = low_refs[0][...]
        for ref in low_refs[1:]:
            low = low + ref[...]
        card_ref[...] = jnp.concatenate(
            [
                low[:rank],
                ids_ref[...].astype(F32),
                jnp.zeros((OWN_MAX * rank - rank - cores, rows), F32),
            ],
            axis=0,
        ).astype(BF16)
        low_out = low[rank:].astype(BF16)
        low_ref[...] = low_out
        core = core_ref[0]
        slot = slot_row(ids_ref[pl.ds(core, 1), :], slot_ref, adapters)
        for s in range(slots):
            part = jnp.where(slot == s, low_out.astype(F32), 0.0)
            spread_ref[s * rank : (s + 1) * rank] = part.astype(BF16)
        for ref, part in ((mine_ref, core), (away_ref, 1 - core)):
            at = pl.ds(pl.multiple_of(part * half, 128), half)
            ref[...] = dot_plain(spread_ref[...], x_ref[:, at]).astype(BF16)

    wide = array((slots * rank, half), BF16)
    shapes = [array((OWN_MAX * rank, rows), BF16), array((rank, rows), BF16), wide, wide]
    scratch = [pltpu.VMEM((slots * rank, rows), BF16)]
    args = [owner_slot, core, ids, x, *lows]
    return call(body, shapes, args, {0: SMEM, 1: SMEM}, scratch=scratch)


def chip_sums(place, card, mine, got, n):
    deep, half, rows = mine.shape[0] // n, mine.shape[1], card.shape[1]
    top = n // 2

    def body(place_ref, card_ref, mine_ref, got_ref, *outs):
        for s in range(n):
            at = pl.ds(pl.multiple_of((place_ref[0] ^ s) * deep, 16), deep)
            total = (mine_ref[at].astype(F32) + got_ref[at].astype(F32)).astype(BF16)
            if s < top:
                outs[s][...] = total
            else:
                outs[top][:, (s - top) * half : (s - top + 1) * half] = total
        outs[top][:, top * half :] = card_ref[...]

    shapes = [array((deep, half), BF16)] * top + [array((deep, top * half + rows), BF16)]
    return list(call(body, shapes, [place, card, mine, got], {0: SMEM}))


def lift_up(owner_slot, core, place, cards, blocks, rank):
    n, adapters = len(blocks), owner_slot.shape[0]
    width = blocks[0].shape[1]
    half = width // 2

    def body(slot_ref, core_ref, place_ref, *refs):
        card_refs, block_refs, outs = refs[:n], refs[n : 2 * n], refs[2 * n :]
        core, first = core_ref[0], place_ref[0] * OWN_MAX
        lifts = []
        for ref in card_refs:
            card = ref[...].astype(F32)
            ids = jnp.where(core == 0, card[rank : rank + 1], card[rank + 1 : rank + 2])
            slot = slot_row(ids.astype(jnp.int32), slot_ref, adapters)
            lift = [jnp.where(slot == first + o, card[:rank], 0.0) for o in range(OWN_MAX)]
            lifts.append(jnp.concatenate(lift, axis=0).astype(BF16))
        if half % 128:
            outs[0][...] = sum(dot_plain(a, b[...]) for a, b in zip(lifts, block_refs))
            return
        for ref, part in zip(outs, (core, 1 - core)):
            at = pl.ds(pl.multiple_of(part * half, 128), half)
            ref[...] = sum(dot_plain(a, b[:, at]) for a, b in zip(lifts, block_refs))

    deep = OWN_MAX * rank
    shapes = [array((deep, width), F32)] if half % 128 else [array((deep, half), F32)] * 2
    args = [owner_slot, core, place, *cards, *blocks]
    out = call(body, shapes, args, {0: SMEM, 1: SMEM, 2: SMEM})
    if half % 128:
        at = core[0] * half
        return [lax.dynamic_slice_in_dim(out[0], p, half, 1) for p in (at, half - at)]
    return out


def adapter_rows(core, ids, low_out, down_t):
    rows, width = ids.shape[1], down_t.shape[1]
    adapters = down_t.shape[0] // low_out.shape[0]

    def body(core_ref, ids_ref, low_ref, down_ref, out_ref, column_ref):
        own_ids = ids_ref[pl.ds(core_ref[0], 1), :]
        low = low_ref[...].astype(F32)
        spread = [jnp.where(own_ids == a, low, 0.0) for a in range(adapters)]
        spread = jnp.concatenate(spread, axis=0).T.astype(BF16)
        out_ref[...] = ADAPTER_SCALE * dot_plain(spread, down_ref[...])
        column_ref[...] = jnp.broadcast_to(own_ids.astype(F32), (rows, rows)).T

    shapes = [array((rows, width), F32), array((rows, rows), F32)]
    return call(body, shapes, [core, ids, low_out, down_t], {0: SMEM})


def finish(weight, id_column, term, pieces, offsets, starts, into=None):
    count = len(pieces)

    def body(*refs):
        weight_ref, column_ref, *refs = refs
        offset_refs, term_ref = refs[:count], refs[count]
        piece_refs = refs[count + 1 : 2 * count + 1]
        out_ref, *held = refs[len(refs) - count - 2 : -1]
        sems = refs[-1]
        own_ids = column_ref[:, :1]
        scale = jnp.zeros(own_ids.shape, F32)
        for a in range(weight.shape[1]):
            scale = jnp.where(own_ids == a, weight_ref[:, a : a + 1], scale)
        copies = []
        for i, (piece, start) in enumerate(zip(pieces, starts)):
            own, chunk = slice(start, start + piece.shape[0]), piece.shape[1]
            at = pl.ds(pl.multiple_of(offset_refs[i][0], 128), chunk)
            total = piece_refs[i][...].astype(F32) + term_ref[own, at]
            held[i][...] = (scale[own] * total).astype(BF16)
            copies.append(pltpu.make_async_copy(held[i], out_ref.at[own, at], sems.at[i]))
            copies[-1].start()
        for copy in copies:
            copy.wait()

    args = [weight, id_column, *offsets, term, *pieces]
    specs = {i: SMEM for i in range(2, 2 + count)}
    aliases = None
    if into is not None:
        specs[len(args)] = ANY
        aliases = {len(args): 0}
        args.append(into)
    scratch = [pltpu.VMEM(p.shape, BF16) for p in pieces] + [pltpu.SemaphoreType.DMA((count,))]
    shape = array(term.shape, BF16)
    return call(body, shape, args, specs, out_specs=ANY, scratch=scratch, aliases=aliases)


def swap(value, axis, step):
    size = lax.axis_size(axis)
    return lax.ppermute(value, axis, [(i, i ^ step) for i in range(size)])


def pick(value, index):
    return lax.dynamic_index_in_dim(value, index, 0, keepdims=False)


def choose(values, index):
    out = values[0]
    for i in range(1, len(values)):
        out = jnp.where(index == i, values[i], out)
    return out


def after(value, *others):
    return lax.optimization_barrier((value, *others))[0]


def local(x, g, ids, owner_slot, w, down, up):
    rows = x.shape[0]
    adapters = owner_slot.shape[0]
    rank = up.shape[1]
    n, tensors, cores = lax.axis_size("dp"), lax.axis_size("tensor"), lax.axis_size("seq")
    z, t, c = lax.axis_index("dp"), lax.axis_index("tensor"), lax.axis_index("seq")
    core, place = one(c), one(z)
    slots = n * OWN_MAX
    labels = jnp.arange(adapters, dtype=jnp.int32)
    ids = ids.reshape(cores, rows)

    top = n // 2
    blocks = {0: g, top: swap(g, "dp", top)}

    def hand_on(froms, *ready):
        bit = top // 2
        while bit:
            for s in [s for s in blocks if s in froms]:
                blocks[s ^ bit] = swap(after(blocks[s], *ready), "dp", bit)
            bit //= 2

    hand_on(range(top))

    w_other = swap(w, "seq", 1)
    width = cores * w.shape[0]
    chunk = width // tensors
    first = None
    if tensors == cores:
        w_parts, first = [w, w_other], one(t ^ c)
    else:
        w_chip = jnp.where(c == 0, jnp.stack([w, w_other]), jnp.stack([w_other, w]))
        w_chip = w_chip.reshape(tensors, chunk, -1)
        w_parts = [pick(w_chip, t ^ k) for k in range(tensors)]

    parts, totals = {}, {}

    def product(s, *ready):
        made = multiply(after(blocks[s], *ready), w_parts, first)
        kept = made[0].astype(F32)
        for k in range(1, tensors):
            kept = kept + swap(made[k], "tensor", k).astype(F32)
        parts[s], totals[s] = made, kept.astype(BF16)

    down_t = down.transpose(1, 2, 0).reshape(adapters * rank, -1)
    up_t = up.reshape(adapters * rank, -1)
    low = project(core, after(ids, w_other), x, g, down_t, up_t, rank)
    lows = [low] + [swap(low, "tensor", s) for s in range(1, tensors)]

    product(0, low)
    card, low_out, mine, away = lift_down(owner_slot, core, ids, x, lows, slots)
    half = mine.shape[1]
    got = swap(after(away, blocks[top]), "seq", 1)
    *held, letter = chip_sums(place, card, mine, got, n)
    cards = {0: card}

    def post(bit, letter):
        known = list(cards)
        got = swap(letter, "dp", bit)
        for s in range(bit):
            total = held[s].astype(F32) + got[:, s * half : (s + 1) * half].astype(F32)
            held[s] = total.astype(BF16) if bit > 1 else total
        for i, s in enumerate(known):
            at = bit * half + i * rows
            cards[s ^ bit] = got[:, at : at + rows]

    post(top, letter)
    term, id_column = adapter_rows(core, ids, low_out, down_t)
    hand_on(range(top, n), card, *parts[0])
    order = [*range(top, n - 1), *range(1, top)]
    ready = [letter]
    for s in order:
        product(s, *ready)
        ready = parts[s]
    last = after(blocks[n - 1], *ready, totals[order[0]])
    away_parts = multiply(last, w_parts, first, range(1, tensors), CUTS)
    kept_parts = multiply(after(last, *away_parts), w_parts, first, (0,), CUTS)
    finals = []
    for j in range(CUTS):
        kept = after(kept_parts[j], *finals).astype(F32)
        for k in range(1, tensors):
            kept = kept + swap(away_parts[(k - 1) * CUTS + j], "tensor", k).astype(F32)
        finals.append(kept.astype(BF16))
    bit = top // 2
    while bit:
        letter = held[bit : 2 * bit] + [cards[s] for s in cards]
        post(bit, after(jnp.concatenate(letter, axis=1), finals[-1]))
        bit //= 2
    cards = [after(cards[s], finals[-1]) for s in range(n)]
    down_sum = after(held[0], finals[-1])
    all_ids = jnp.stack([v[rank : rank + cores] for v in cards]).astype(jnp.int32)
    counts = jnp.sum((all_ids.reshape(1, -1) == labels[:, None]).astype(F32), axis=1)
    weight = F32(n * cores * rows) / (F32(adapters) * counts)
    my_slots = z * OWN_MAX + jnp.arange(OWN_MAX, dtype=jnp.int32)
    slot_weight = ADAPTER_SCALE * jnp.sum(
        jnp.where(owner_slot[None, :] == my_slots[:, None], weight[None, :], 0.0), axis=1
    )
    down_grad = down_sum.reshape(OWN_MAX, rank, half) * slot_weight[:, None, None]
    down_grad = down_grad.transpose(2, 0, 1)

    back = [swap(totals[s], "dp", s) if s else totals[0] for s in range(n - 1)]
    last_back = [swap(v, "dp", n - 1) for v in finals]
    span = n // tensors
    low_bits, high_bits = z % span, z // span
    pieces, offsets, starts = [], [], []
    for r in range(span):
        for j in range(CUTS if r == span - 1 else 1):
            choices = [back[s] for s in range(r, n - 1, span)]
            start = j * (rows // CUTS)
            if r == span - 1:
                choices = [v[start : start + rows // CUTS] for v in choices] + [last_back[j]]
            choices[0] = after(choices[0], finals[-1], *(choices_before if j else ()))
            choices_before = choices
            for k in range(tensors):
                piece = choose(choices, t ^ k ^ high_bits)
                pieces.append(swap(piece, "tensor", k) if k else piece)
                offsets.append((r ^ low_bits) * width + (t ^ k) * chunk)
                starts.append(start)
    if chunk % 128 == 0:
        offsets = [one(v) for v in offsets]
        args = (weight[None, :], id_column, term)
        late = len(pieces) - len(pieces)
        early = finish(*args, pieces[:late], offsets[:late], starts[:late]) if late else None
        input_gradient = finish(*args, pieces[late:], offsets[late:], starts[late:], into=early)
    else:
        base = jnp.zeros((rows, span * width), BF16)
        for piece, offset, start in zip(pieces, offsets, starts):
            base = lax.dynamic_update_slice(base, piece, (start, offset))
        own_match = (pick(ids, c)[:, None] == labels[None, :]).astype(F32)
        own_weight = jnp.sum(own_match * weight[None, :], axis=1)
        input_gradient = (own_weight[:, None] * (base.astype(F32) + term)).astype(BF16)

    up_mine, up_away = lift_up(
        owner_slot, core, place, cards, [blocks[s] for s in range(n)], rank
    )
    up_sum = up_mine + swap(up_away, "seq", 1)
    up_grad = up_sum.reshape(OWN_MAX, rank, -1) * slot_weight[:, None, None]
    return input_gradient, down_grad, up_grad


def solution(mesh):
    in_specs = (
        P(("groups", "dp", "seq"), "tensor"),
        P(("groups", "dp", "seq"), "tensor"),
        P(("groups", "dp")),
        P("groups"),
        P(("dp", "seq"), "tensor"),
        P(("groups", "tensor"), None, None),
        P("groups", None, "tensor"),
    )
    out_specs = (
        P(("groups", "dp", "seq"), "tensor"),
        P(("groups", "tensor", "seq"), "dp", None),
        P(("groups", "dp"), None, ("tensor", "seq")),
    )
    return jax.shard_map(local, mesh=mesh, in_specs=in_specs, out_specs=out_specs, check_vma=False)
```
